32 devices in a mesh: grp: 2 (over x), chan: 16 (over z, y, core).
Axes of the slice: x: 2, y: 2, z: 4, core: 2. Of those that a mesh axis runs over, the one named last changes fastest.
Arguments:
- voltages: bfloat16 [8192, 2, 64, 128], P(('grp', 'chan')), parts along dimension 0, may hold values from -9 to 9
- delays: float32 [512, 64], replicated, may hold values from -2 to 2
- pointing: int32 [32], P('grp'), parts along dimension 0, may hold values from 0 to 511
- dm_index: int32 [32], P(('grp', 'chan')), parts along dimension 0, may hold values from 0 to 511
- dish_mask: int32 [128], P('grp'), parts along dimension 0, may hold values 0 or 1
Outputs:
- dedispersed: float32 [32, 2, 128, 4096], P(('grp', 'chan')), parts along dimension 0
The draws below stay inside these ranges and needn't reach their ends.
There are 2 independent parts, one for each index of `grp`. The reference program is written for one: setup_inputs(seed, part) draws one part's arguments, and reference() takes and returns one part's arrays. A program takes and returns all parts, laid end to end along the dimension named above; an argument that names none is the same for every part. Nothing has to cross between parts.
All inputs are finite; a program needn't handle non-finite values.
Results may differ from the reference program's by a relative error of at most 0.005.
Values may be sent and summed in bfloat16 or wider, within the bound.
No kernel may reach another device: no remote copies, remote signals or barrier semaphores. Data moves between devices by JAX's collectives and lax.ppermute only.
A program may use at most 64 MiB of HBM per device.

```python
import math
import jax
import jax.numpy as jnp
from jax import lax

DISH = 64
CHANS = 4096
TIME = 128
LOG_LEN = 19
POINTINGS = 512
DM_TRIALS = 512
BEAMS = 16


def draw_voltages(key, part):
    base_key, rough_key = jax.random.split(key)
    array_shape = (CHANS, 2, DISH, TIME)
    channel = jnp.arange(CHANS, dtype=jnp.float32)
    roughness = jnp.exp(jax.random.uniform(rough_key, (CHANS,), minval=-0.25, maxval=0.25))
    base_draw = jnp.clip(jax.random.normal(base_key, array_shape), -4.0, 4.0)
    ramp_scale = 1.0 + 2.0 * channel / (CHANS - 1)
    chan_scale = jnp.sqrt(ramp_scale) * roughness
    return (base_draw * chan_scale[:, None, None, None]).astype(jnp.bfloat16)


def touch_ends(result, rng, low, largest):
    place = [jax.random.randint(jax.random.fold_in(rng, axis), (), 0, length) for axis, length in enumerate(result.shape)]
    widest = result.shape.index(max(result.shape))
    neighbour = place[:widest] + [(place[widest] + 1) % result.shape[widest]] + place[widest + 1:]
    return result.at[tuple(place)].set(low).at[tuple(neighbour)].set(largest)


def setup_inputs(seed: int = 0, part: int = 0) -> dict:
    key_list = jax.random.split(jax.random.key(seed), 6)
    part_splits = jax.random.split(jax.random.fold_in(key_list[5], part), 6)
    return {
        "voltages": draw_voltages(jax.random.fold_in(jax.random.fold_in(key_list[5], part), 71), part),
        "delays": jnp.clip(jax.random.uniform(key_list[1], (POINTINGS, DISH), jnp.float32, -2.0, 2.0), -2.0, 2.0),
        "pointing": touch_ends(jax.random.randint(part_splits[2], (BEAMS,), 0, POINTINGS), jax.random.fold_in(part_splits[2], 1), 0, POINTINGS - 1).astype(jnp.int32),
        "dm_index": touch_ends(jax.random.randint(part_splits[3], (BEAMS,), 0, DM_TRIALS), jax.random.fold_in(part_splits[3], 1), 0, DM_TRIALS - 1).astype(jnp.int32),
        "dish_mask": touch_ends((jax.random.randint(part_splits[4], (DISH,), 0, 8) < 7).astype(jnp.int32), jax.random.fold_in(part_splits[4], 1), 0, 1),
    }


TWO_PI = 2.0 * math.pi
BAND_LOW = 0.856
BAND_WIDTH = 0.856
EPSILON = 1e-06

def rounded(values):
    return lax.optimization_barrier(values.astype(jnp.bfloat16)).astype(jnp.float32)

def chirp_index(freq_index, rate):
    length = 2 ** LOG_LEN
    radix_len = 2 ** ((LOG_LEN + 1) // 2)
    high_part = freq_index // radix_len
    low_part = freq_index % radix_len
    squared = (2 * high_part * low_part % (length // radix_len) * radix_len + low_part * low_part) % length
    return rate * squared % length

def reference(voltages, delays, pointing, dm_index, dish_mask):
    length = TIME * CHANS
    channel = jnp.arange(CHANS, dtype=jnp.int32)
    frequency = BAND_LOW + BAND_WIDTH * (channel.astype(jnp.float32) + 0.5) / CHANS
    dish_gain = dish_mask.astype(jnp.float32) / math.sqrt(DISH)
    volt_rows = voltages.astype(jnp.float32).reshape(CHANS, 2 * DISH, TIME)
    freq_index = jnp.arange(length, dtype=jnp.int32)

    def one_beam(beam_item):
        pointing_row, trial_index = beam_item
        delay_row = delays[pointing_row]
        phase_all = (TWO_PI * frequency)[:, None] * delay_row[None, :]
        weight_re = rounded(jnp.cos(phase_all) * dish_gain)
        weight_im = rounded(-jnp.sin(phase_all) * dish_gain)
        row_re = jnp.concatenate([weight_re, -weight_im], 1)
        row_im = jnp.concatenate([weight_im, weight_re], 1)
        stacked = jnp.stack([row_re, row_im], 1)
        formed = rounded(jnp.einsum('cpk,ckt->cpt', stacked, volt_rows))
        mean_power = jnp.sum(formed * formed) / length
        channel_values = formed[:, 0] + 1j * formed[:, 1]
        chan_series = jnp.fft.ifft(channel_values, axis=0) * math.sqrt(CHANS)
        sequence = jnp.transpose(chan_series).reshape(length)
        spectrum = jnp.fft.fft(sequence)
        phase_chirp = -TWO_PI / length * chirp_index(freq_index, 2 * trial_index + 1).astype(jnp.float32)
        series = jnp.fft.ifft(spectrum * (jnp.cos(phase_chirp) + 1j * jnp.sin(phase_chirp)))
        series = series.reshape(TIME, CHANS)
        factor = lax.rsqrt(mean_power + EPSILON)
        return jnp.stack([jnp.real(series) * factor, jnp.imag(series) * factor], 0)
    return lax.map(one_beam, (pointing, dm_index))
```

```python
import functools
import math

import jax
import jax.numpy as jnp
from jax import lax
from jax.experimental import pallas as pl
from jax.experimental.pallas import tpu as pltpu
from jax.sharding import PartitionSpec as P

TWO_PI = 2.0 * math.pi
BAND_LOW = 0.856
BAND_WIDTH = 0.856
EPSILON = 1e-06
F32 = jnp.float32
BF16 = jnp.bfloat16


def cmul(a, b):
    return (a[0] * b[0] - a[1] * b[1], a[0] * b[1] + a[1] * b[0])


def cadd(a, b):
    return (a[0] + b[0], a[1] + b[1])


def csub(a, b):
    return (a[0] - b[0], a[1] - b[1])


def turn(a, num, den):
    num = num % den
    if num == 0:
        return a
    if 2 * num == den:
        return (-a[0], -a[1])
    if 4 * num == den:
        return (-a[1], a[0])
    if 4 * num == 3 * den:
        return (a[1], -a[0])
    if 8 * num % den == 0:
        root = math.sqrt(0.5)
        plus, minus = (a[0] + a[1]) * root, (a[0] - a[1]) * root
        return {1: (minus, plus), 3: (-plus, minus), 5: (-minus, -plus), 7: (plus, -minus)}[
            8 * num // den
        ]
    cosine, sine = math.cos(TWO_PI * num / den), math.sin(TWO_PI * num / den)
    return (a[0] * cosine - a[1] * sine, a[0] * sine + a[1] * cosine)


def fft_list(values, sign):
    points = len(values)
    if points == 1:
        return values
    if points == 2:
        return [cadd(values[0], values[1]), csub(values[0], values[1])]
    quarter = points // 4
    parts = [fft_list(values[i::4], sign) for i in range(4)]
    out = [None] * points
    for k in range(quarter):
        a, b, c, d = [turn(parts[i][k], sign * i * k, points) for i in range(4)]
        s0, s1 = cadd(a, c), csub(a, c)
        s2, s3 = cadd(b, d), turn(csub(b, d), sign, 4)
        out[k] = cadd(s0, s2)
        out[k + quarter] = cadd(s1, s3)
        out[k + 2 * quarter] = csub(s0, s2)
        out[k + 3 * quarter] = csub(s1, s3)
    return out


def beam_kernel(
    chans, comb, point_ref, delay_ref, mask_ref, volt_ref, out_ref, zero_ref, fine_ref, coarse_ref, rows_ref
):
    step = pl.program_id(0)
    part_rows, combs = volt_ref.shape[0], volt_ref.shape[1]
    beams = out_ref.shape[0]
    dishes = delay_ref.shape[0]
    chan_dev = part_rows * comb

    @pl.when(step == 0)
    def _():
        table_rows = delay_ref.shape[1]
        place = lax.broadcasted_iota(jnp.int32, (beams, table_rows), 1)
        which = lax.broadcasted_iota(jnp.int32, (beams, table_rows), 0)
        wanted = jnp.zeros((beams, table_rows), jnp.int32)
        for b in range(beams):
            wanted = jnp.where(which == b, point_ref[b], wanted)
        select = (wanted == place).astype(F32)
        doubled = jnp.concatenate([delay_ref[...], delay_ref[...]], 0)
        tau = lax.dot_general(
            select,
            doubled,
            (((1,), (1,)), ((), ())),
            precision=lax.Precision.HIGHEST,
            preferred_element_type=F32,
        )
        first = lax.axis_index("chan") * chan_dev
        frequency = BAND_LOW + BAND_WIDTH * (first.astype(F32) + 0.5) / chans
        angle = (TWO_PI * frequency) * tau
        gain_half = mask_ref[...].astype(F32) / math.sqrt(dishes)
        gain = jnp.concatenate([gain_half, gain_half], 1)
        cosine, sine = jnp.cos(angle) * gain, jnp.sin(angle) * gain
        left = lax.broadcasted_iota(jnp.int32, (beams, 2 * dishes), 1) < dishes
        zero_ref[0] = jnp.where(left, cosine, sine)
        zero_ref[1] = jnp.where(left, -sine, cosine)
        for table_ref, stride in ((fine_ref, 1), (coarse_ref, comb)):
            shift = (TWO_PI * BAND_WIDTH / chans * stride) * tau
            count = table_ref.shape[0]
            powers = [(jnp.ones_like(tau), jnp.zeros_like(tau)), (jnp.cos(shift), -jnp.sin(shift))]
            for k in range(2, count):
                powers.append(cmul(powers[k // 2], powers[k - k // 2]))
            for k in range(count):
                table_ref[k, 0] = powers[k][0]
                table_ref[k, 1] = powers[k][1]

    group = rows_ref.shape[1] // beams
    for g in range(part_rows * combs // group):
        for i in range(group):
            row = g * group + i
            ja, cb = row % part_rows, row // part_rows
            base = cmul(
                (zero_ref[0], zero_ref[1]),
                (fine_ref[step * combs + cb, 0], fine_ref[step * combs + cb, 1]),
            )
            weight = cmul(base, (coarse_ref[ja, 0], coarse_ref[ja, 1]))
            stacked = jnp.concatenate(weight, 0).astype(BF16)
            formed = jnp.dot(stacked, volt_ref[ja, cb], preferred_element_type=F32)
            rows_ref[0, pl.ds(i, beams, stride=group), :] = formed[:beams]
            rows_ref[1, pl.ds(i, beams, stride=group), :] = formed[beams:]
        samples = rows_ref.shape[2]
        for p in range(2):
            out_ref[:, g * group : (g + 1) * group, p * samples : (p + 1) * samples] = (
                rows_ref[p].reshape(beams, group, samples).astype(BF16)
            )


def form_beams(voltages, delays, pointing, dish_mask, chans, comb):
    chan_dev, _, dishes, samples = voltages.shape
    beams = pointing.shape[0]
    part_rows = chan_dev // comb
    combs = max(2, 16 // part_rows)
    group = 16
    volt = voltages.reshape(part_rows, comb, 2 * dishes, samples)
    return pl.pallas_call(
        functools.partial(beam_kernel, chans, comb),
        out_shape=jax.ShapeDtypeStruct((beams, chan_dev, 2 * samples), BF16),
        grid=(comb // combs,),
        in_specs=[
            pl.BlockSpec(memory_space=pltpu.SMEM),
            pl.BlockSpec((dishes, delays.shape[0]), lambda i: (0, 0)),
            pl.BlockSpec((1, dishes), lambda i: (0, 0)),
            pl.BlockSpec((part_rows, combs, 2 * dishes, samples), lambda i: (0, i, 0, 0)),
        ],
        out_specs=pl.BlockSpec((beams, part_rows * combs, 2 * samples), lambda i: (0, i, 0)),
        scratch_shapes=[
            pltpu.VMEM((2, beams, 2 * dishes), F32),
            pltpu.VMEM((comb, 2, beams, 2 * dishes), F32),
            pltpu.VMEM((part_rows, 2, beams, 2 * dishes), F32),
            pltpu.VMEM((2, beams * group, samples), F32),
        ],
        compiler_params=pltpu.CompilerParams(vmem_limit_bytes=40 * 2**20),
        name="form_beams",
    )(pointing, delays.T, dish_mask.reshape(1, dishes), volt)


def phasor(phase, points):
    half = points // 2
    angle = (TWO_PI / points) * ((phase + half) % points - half).astype(F32)
    return jnp.stack([jnp.cos(angle), jnp.sin(angle)], 0)


def chirp_tables(rate, samples, chans):
    length = samples * chans
    low, comb = 2 * samples, chans // (2 * samples)
    f = jnp.arange(samples, dtype=jnp.int32)[None, :]
    shift = 2 * rate * f % chans
    shift_low, shift_high = shift % low, shift // low
    inverse = rate * (2 - rate * rate) % (2 * comb)
    m = jnp.arange(comb, dtype=jnp.int32)[:, None]
    unit = length // (2 * comb)
    c_a = jnp.arange(samples, dtype=jnp.int32)[:, None]
    turn_a = phasor(-(rate * c_a * f % samples), samples)
    turn_b = phasor(-(rate * m * f % (chans // 2)), chans // 2)
    quad = inverse * m * m % (2 * comb) * unit
    before = [phasor(quad - (m - shift_high - beta) % comb * low * f, length) for beta in range(2)]
    place = rate * m % comb
    quad = inverse * place * place % (2 * comb) * unit
    gauss_phase = -(rate * m * m % (2 * comb)) * unit
    gauss = jnp.sum(phasor(gauss_phase, length), axis=1)
    scale = 2 * samples / (length * math.sqrt(chans))
    after = []
    for beta in range(2):
        turned = phasor(
            quad + low * place * f + f * (shift_low - low * beta) - rate * f * f % length, length
        )
        real, imag = cmul((turned[0], turned[1]), (gauss[0] * scale, gauss[1] * scale))
        after.append(jnp.stack([real, imag], 0))
    return turn_a, turn_b, jnp.stack(before), jnp.stack(after), shift_low


def transforms(samples, chans):
    low, comb = 2 * samples, chans // (2 * samples)
    t = jnp.arange(samples, dtype=jnp.int32)
    cosine, sine = phasor(t[:, None] * t[None, :] % samples, samples)
    time_mat = jnp.concatenate(
        [jnp.concatenate([cosine, -sine], 1), jnp.concatenate([sine, cosine], 1)], 0
    )
    n = jnp.arange(low, dtype=jnp.int32)
    c_b = jnp.arange(comb, dtype=jnp.int32)
    product = (comb * n[None, None, :] + c_b[:, None, None]) * n[None, :, None] % chans
    cosine, sine = phasor(product, chans)
    return time_mat.astype(BF16), jnp.concatenate([cosine, sine], 1).astype(BF16)


def dedisperse_kernel(
    chans, first_steps,
    rate_ref, beam_ref, time_ref, mix_ref, turn_a_ref, turn_b_ref, before_ref, after_ref, shift_ref,
    out_ref, grid_ref, power_ref, scaled_ref,
):
    step = pl.program_id(0)
    samples = turn_a_ref.shape[1]
    low, comb = 2 * samples, grid_ref.shape[0]
    combs = beam_ref.shape[1]

    @pl.when(step == 0)
    def _():
        power_ref[...] = jnp.zeros_like(power_ref)

    @pl.when(step < first_steps)
    def _():
        for i in range(combs):
            beam = beam_ref[:, i].reshape(low, 2 * samples)
            wide = beam.astype(F32)
            power_ref[...] += jnp.sum((wide * wide).reshape(low // 8, 8, 2 * samples), 0)
            spectrum = jnp.dot(beam, time_ref[...], preferred_element_type=F32)
            comb_row = step * combs + i
            turned = cmul(
                (turn_a_ref[0], turn_a_ref[1]),
                (turn_b_ref[0, pl.ds(comb_row, 1), :], turn_b_ref[1, pl.ds(comb_row, 1), :]),
            )
            halves = []
            for h in range(2):
                piece = spectrum[h * samples : (h + 1) * samples]
                moved = cmul((piece[:, :samples], piece[:, samples:]), turned)
                halves.append(jnp.concatenate(moved, 1).astype(BF16))
            mixed = jnp.dot(
                mix_ref[i], jnp.concatenate(halves, 0), preferred_element_type=F32
            )
            grid_ref[comb_row, 0] = mixed[:low, :samples] - mixed[low:, samples:]
            grid_ref[comb_row, 1] = mixed[:low, samples:] + mixed[low:, :samples]

    @pl.when(step == first_steps)
    def _():
        mean_power = jnp.sum(power_ref[...]) / (samples * chans)
        factor = lax.rsqrt(jnp.full((1, samples), mean_power, F32) + EPSILON)
        for beta in range(2):
            for p in range(2):
                scaled_ref[beta, p] = after_ref[beta, p] * factor
        rate = 2 * rate_ref[0] + 1

        @pl.loop(0, low // 8)
        def _(tile):
            rows = pl.ds(pl.multiple_of(tile * 8, 8), 8)
            values = [(grid_ref[c, 0, rows, :], grid_ref[c, 1, rows, :]) for c in range(comb)]
            values = fft_list(values, 1)
            position = tile * 8 + lax.broadcasted_iota(jnp.int32, (8, samples), 0)
            wrapped = position < shift_ref[...]
            for m in range(comb):
                table = [
                    jnp.where(wrapped, before_ref[1, p, m : m + 1, :], before_ref[0, p, m : m + 1, :])
                    for p in range(2)
                ]
                values[m] = cmul(values[m], table)
            values = fft_list(values, -1)
            for k in range(comb):
                table = [
                    jnp.where(wrapped, scaled_ref[1, p, k : k + 1, :], scaled_ref[0, p, k : k + 1, :])
                    for p in range(2)
                ]
                real, imag = cmul(values[k], table)
                place = lax.rem(rate * k, comb)
                grid_ref[place, 0, rows, :] = real
                grid_ref[place, 1, rows, :] = imag

    @pl.when(step >= first_steps)
    def _():
        per = out_ref.shape[3] // low
        for i in range(per):
            high = (step - first_steps) * per + i
            both = jnp.concatenate([grid_ref[high, 0], grid_ref[high, 1]], 1).astype(BF16)
            result = lax.dot_general(
                time_ref[...], both, (((1,), (1,)), ((), ())), preferred_element_type=F32
            )
            out_ref[0, 0, :, i * low : (i + 1) * low] = result[:samples]
            out_ref[0, 1, :, i * low : (i + 1) * low] = result[samples:]


def dedisperse(beam, trial, samples, chans):
    low, comb = 2 * samples, chans // (2 * samples)
    tables = chirp_tables(2 * trial[0] + 1, samples, chans)
    time_mat, mix = transforms(samples, chans)
    devices, _, part_rows, width = beam.shape
    combs, first_steps, last_steps = 2, comb // 2, 4

    def early(i):
        return jnp.minimum(i, first_steps - 1)

    def whole(array):
        return pl.BlockSpec(array.shape, lambda i: (0,) * array.ndim)

    return pl.pallas_call(
        functools.partial(dedisperse_kernel, chans, first_steps),
        out_shape=jax.ShapeDtypeStruct((1, 2, samples, chans), F32),
        grid=(first_steps + last_steps,),
        in_specs=[
            pl.BlockSpec(memory_space=pltpu.SMEM),
            pl.BlockSpec((devices, combs, part_rows, width), lambda i: (0, early(i), 0, 0)),
            whole(time_mat),
            pl.BlockSpec((combs, 2 * low, low), lambda i: (early(i), 0, 0)),
        ]
        + [whole(table) for table in tables],
        out_specs=pl.BlockSpec(
            (1, 2, samples, chans // last_steps),
            lambda i: (0, 0, 0, jnp.maximum(i - first_steps, 0)),
        ),
        scratch_shapes=[
            pltpu.VMEM((comb, 2, low, samples), F32),
            pltpu.VMEM((8, 2 * samples), F32),
            pltpu.VMEM((2, 2, comb, samples), F32),
        ],
        compiler_params=pltpu.CompilerParams(vmem_limit_bytes=40 * 2**20),
        name="dedisperse",
    )(trial, beam, time_mat, mix, *tables)


def on_device(chan_devs, voltages, delays, pointing, dm_index, dish_mask):
    chan_dev, _, _, samples = voltages.shape
    chans = chan_dev * chan_devs
    comb = chans // (2 * samples)
    beam_dev = dm_index.shape[0]
    formed = form_beams(voltages, delays, pointing, dish_mask, chans, comb)
    formed = lax.all_to_all(formed, "chan", split_axis=0, concat_axis=0, tiled=True)
    part_rows = chan_dev // comb
    formed = formed.reshape(chan_devs, beam_dev, comb, part_rows, 2 * samples)
    if part_rows % 16:
        formed = jnp.transpose(formed, (1, 2, 0, 3, 4)).reshape(
            1, beam_dev, comb, chans // comb, 2 * samples
        )
    pieces = [
        dedisperse(formed[:, b], dm_index[b : b + 1], samples, chans) for b in range(beam_dev)
    ]
    return pieces[0] if beam_dev == 1 else jnp.concatenate(pieces, 0)


def solution(mesh):
    return jax.shard_map(
        functools.partial(on_device, mesh.shape["chan"]),
        mesh=mesh,
        in_specs=(
            P(("grp", "chan"), None, None, None),
            P(),
            P("grp"),
            P(("grp", "chan")),
            P("grp"),
        ),
        out_specs=P(("grp", "chan"), None, None, None),
        check_vma=False,
    )
```

```python
import functools
import math

import jax
import jax.numpy as jnp
from jax import lax
from jax.experimental import pallas as pl
from jax.experimental.pallas import tpu as pltpu
from jax.sharding import PartitionSpec as P

TWO_PI = 2.0 * math.pi
BAND_LOW = 0.856
BAND_WIDTH = 0.856
EPSILON = 1e-06
F32 = jnp.float32
BF16 = jnp.bfloat16


def cmul(a, b):
    return (a[0] * b[0] - a[1] * b[1], a[0] * b[1] + a[1] * b[0])


def cadd(a, b):
    return (a[0] + b[0], a[1] + b[1])


def csub(a, b):
    return (a[0] - b[0], a[1] - b[1])


def turn(a, num, den):
    num = num % den
    if num == 0:
        return a
    if 2 * num == den:
        return (-a[0], -a[1])
    if 4 * num == den:
        return (-a[1], a[0])
    if 4 * num == 3 * den:
        return (a[1], -a[0])
    if 8 * num % den == 0:
        root = math.sqrt(0.5)
        plus, minus = (a[0] + a[1]) * root, (a[0] - a[1]) * root
        return {1: (minus, plus), 3: (-plus, minus), 5: (-minus, -plus), 7: (plus, -minus)}[
            8 * num // den
        ]
    cosine, sine = math.cos(TWO_PI * num / den), math.sin(TWO_PI * num / den)
    return (a[0] * cosine - a[1] * sine, a[0] * sine + a[1] * cosine)


def fft_list(values, sign):
    points = len(values)
    if points == 1:
        return values
    if points == 2:
        return [cadd(values[0], values[1]), csub(values[0], values[1])]
    quarter = points // 4
    parts = [fft_list(values[i::4], sign) for i in range(4)]
    out = [None] * points
    for k in range(quarter):
        a, b, c, d = [turn(parts[i][k], sign * i * k, points) for i in range(4)]
        s0, s1 = cadd(a, c), csub(a, c)
        s2, s3 = cadd(b, d), turn(csub(b, d), sign, 4)
        out[k] = cadd(s0, s2)
        out[k + quarter] = cadd(s1, s3)
        out[k + 2 * quarter] = csub(s0, s2)
        out[k + 3 * quarter] = csub(s1, s3)
    return out


def beam_kernel(
    chans, comb, point_ref, delay_hbm, mask_hbm, volt_hbm, out_hbm,
    delay_ref, mask_ref, volt_ref, out_ref, zero_ref, fine_ref, coarse_ref, rows_ref,
    small_sem, volt_sem, out_sem,
):
    part_rows = volt_ref.shape[0]
    beams = out_ref.shape[0]
    dishes = delay_ref.shape[0]
    samples = rows_ref.shape[3]
    chan_dev = part_rows * comb
    group = rows_ref.shape[2] // beams
    group_combs = group // part_rows
    groups = chan_dev // group

    def volt_copy(g):
        combs = pl.ds(g * group_combs, group_combs)
        return pltpu.make_async_copy(volt_hbm.at[:, combs], volt_ref.at[:, combs], volt_sem.at[g])

    def out_copy(g):
        rows = pl.ds(pl.multiple_of(g * group, group), group)
        return pltpu.make_async_copy(out_ref.at[:, rows], out_hbm.at[:, rows], out_sem.at[g])

    delay_copy = pltpu.make_async_copy(delay_hbm, delay_ref, small_sem.at[0])
    mask_copy = pltpu.make_async_copy(mask_hbm, mask_ref, small_sem.at[1])
    delay_copy.start()
    mask_copy.start()
    for g in range(groups):
        volt_copy(g).start()
    delay_copy.wait()
    mask_copy.wait()

    table_rows = delay_ref.shape[1]
    place = lax.broadcasted_iota(jnp.int32, (beams, table_rows), 1)
    which = lax.broadcasted_iota(jnp.int32, (beams, table_rows), 0)
    wanted = jnp.zeros((beams, table_rows), jnp.int32)
    for b in range(beams):
        wanted = jnp.where(which == b, point_ref[b], wanted)
    select = (wanted == place).astype(F32)
    doubled = jnp.concatenate([delay_ref[...], delay_ref[...]], 0)
    tau = lax.dot_general(
        select,
        doubled,
        (((1,), (1,)), ((), ())),
        precision=lax.Precision.HIGHEST,
        preferred_element_type=F32,
    )
    first = lax.axis_index("chan") * chan_dev
    frequency = BAND_LOW + BAND_WIDTH * (first.astype(F32) + 0.5) / chans
    angle = (TWO_PI * frequency) * tau
    gain_half = mask_ref[...].astype(F32) / math.sqrt(dishes)
    gain = jnp.concatenate([gain_half, gain_half], 1)
    cosine, sine = jnp.cos(angle) * gain, jnp.sin(angle) * gain
    left = lax.broadcasted_iota(jnp.int32, (beams, 2 * dishes), 1) < dishes
    zero_ref[0] = jnp.where(left, cosine, sine)
    zero_ref[1] = jnp.where(left, -sine, cosine)
    for table_ref, stride in ((fine_ref, 1), (coarse_ref, comb)):
        shift = (TWO_PI * BAND_WIDTH / chans * stride) * tau
        count = table_ref.shape[0]
        powers = [(jnp.ones_like(tau), jnp.zeros_like(tau)), (jnp.cos(shift), -jnp.sin(shift))]
        for k in range(2, count):
            powers.append(cmul(powers[k // 2], powers[k - k // 2]))
        for k in range(count):
            table_ref[k, 0] = powers[k][0]
            table_ref[k, 1] = powers[k][1]

    @pl.loop(0, groups)
    def _(g):
        volt_copy(g).wait()
        slot = g % 2
        for i in range(group):
            ja, cb = i % part_rows, g * group_combs + i // part_rows
            if ja == 0:
                base = cmul((zero_ref[0], zero_ref[1]), (fine_ref[cb, 0], fine_ref[cb, 1]))
            weight = cmul(base, (coarse_ref[ja, 0], coarse_ref[ja, 1]))
            stacked = jnp.concatenate(weight, 0).astype(BF16)
            formed = jnp.dot(stacked, volt_ref[ja, cb], preferred_element_type=F32)
            rows_ref[slot, 0, pl.ds(i, beams, stride=group), :] = formed[:beams]
            rows_ref[slot, 1, pl.ds(i, beams, stride=group), :] = formed[beams:]
        rows = pl.ds(pl.multiple_of(g * group, group), group)
        for p in range(2):
            out_ref[:, rows, p * samples : (p + 1) * samples] = (
                rows_ref[slot, p].reshape(beams, group, samples).astype(BF16)
            )
        out_copy(g).start()

    for g in range(groups):
        out_copy(g).wait()


def form_beams(voltages, delays, pointing, dish_mask, chans, comb):
    chan_dev, _, dishes, samples = voltages.shape
    beams = pointing.shape[0]
    part_rows = chan_dev // comb
    group = part_rows * max(1, 16 // part_rows)
    hbm = pl.BlockSpec(memory_space=pltpu.HBM)
    volt = voltages.reshape(part_rows, comb, 2 * dishes, samples)
    return pl.pallas_call(
        functools.partial(beam_kernel, chans, comb),
        out_shape=jax.ShapeDtypeStruct((beams, chan_dev, 2 * samples), BF16),
        in_specs=[pl.BlockSpec(memory_space=pltpu.SMEM), hbm, hbm, hbm],
        out_specs=hbm,
        scratch_shapes=[
            pltpu.VMEM((dishes, delays.shape[0]), F32),
            pltpu.VMEM((1, dishes), jnp.int32),
            pltpu.VMEM(volt.shape, BF16),
            pltpu.VMEM((beams, chan_dev, 2 * samples), BF16),
            pltpu.VMEM((2, beams, 2 * dishes), F32),
            pltpu.VMEM((comb, 2, beams, 2 * dishes), F32),
            pltpu.VMEM((part_rows, 2, beams, 2 * dishes), F32),
            pltpu.VMEM((2, 2, beams * group, samples), F32),
            pltpu.SemaphoreType.DMA((2,)),
            pltpu.SemaphoreType.DMA((chan_dev // group,)),
            pltpu.SemaphoreType.DMA((chan_dev // group,)),
        ],
        compiler_params=pltpu.CompilerParams(vmem_limit_bytes=60 * 2**20),
        name="form_beams",
    )(pointing, delays.T, dish_mask.reshape(1, dishes), volt)


def phasor(phase, points):
    half = points // 2
    angle = (TWO_PI / points) * ((phase + half) % points - half).astype(F32)
    return jnp.stack([jnp.cos(angle), jnp.sin(angle)], 0)


def chirp_tables(rate, samples, chans):
    length = samples * chans
    low, comb = 2 * samples, chans // (2 * samples)
    f = jnp.arange(samples, dtype=jnp.int32)[None, :]
    shift = 2 * rate * f % chans
    shift_low, shift_high = shift % low, shift // low
    inverse = rate * (2 - rate * rate) % (2 * comb)
    m = jnp.arange(comb, dtype=jnp.int32)[:, None]
    unit = length // (2 * comb)
    c_a = jnp.arange(samples, dtype=jnp.int32)[:, None]
    turn_a = phasor(-(rate * c_a * f % samples), samples)
    turn_b = phasor(-(rate * m * f % (chans // 2)), chans // 2)
    quad = inverse * m * m % (2 * comb) * unit
    before = [phasor(quad - (m - shift_high - beta) % comb * low * f, length) for beta in range(2)]
    place = rate * m % comb
    quad = inverse * place * place % (2 * comb) * unit
    gauss_phase = -(rate * m * m % (2 * comb)) * unit
    gauss = jnp.sum(phasor(gauss_phase, length), axis=1)
    scale = 2 * samples / (length * math.sqrt(chans))
    after = []
    for beta in range(2):
        turned = phasor(
            quad + low * place * f + f * (shift_low - low * beta) - rate * f * f % length, length
        )
        real, imag = cmul((turned[0], turned[1]), (gauss[0] * scale, gauss[1] * scale))
        after.append(jnp.stack([real, imag], 0))
    return turn_a, turn_b, jnp.stack(before), jnp.stack(after), shift_low


def time_matrix(samples):
    t = jnp.arange(samples, dtype=jnp.int32)
    cosine, sine = phasor(t[:, None] * t[None, :] % samples, samples)
    return jnp.concatenate(
        [jnp.concatenate([cosine, -sine], 1), jnp.concatenate([sine, cosine], 1)], 0
    ).astype(BF16)


def mix_matrices(samples, chans):
    low, comb = 2 * samples, chans // (2 * samples)
    n = jnp.arange(low, dtype=jnp.int32)
    c_b = jnp.arange(comb, dtype=jnp.int32)
    product = (comb * n[None, None, :] + c_b[:, None, None]) * n[None, :, None] % chans
    cosine, sine = phasor(product, chans)
    return jnp.concatenate([cosine, sine], 1).astype(BF16)


def dedisperse_kernel(
    chans, first_steps,
    rate_ref, beam_ref, time_ref, mix_hbm, turn_a_ref, turn_b_ref, before_ref, after_ref, shift_ref,
    out_ref, grid_ref, power_ref, scaled_ref, mix_ref, mix_sem,
):
    step = pl.program_id(0)
    samples = turn_a_ref.shape[1]
    low, comb = 2 * samples, grid_ref.shape[0]
    combs = comb // first_steps

    def mix_copy(c):
        return pltpu.make_async_copy(mix_hbm.at[c], mix_ref.at[c], mix_sem.at[c])

    @pl.when(step == 0)
    def _():
        for c in range(comb):
            mix_copy(c).start()
        power_ref[...] = jnp.zeros_like(power_ref)

    @pl.when(step < first_steps)
    def _():
        for i in range(combs):
            comb_row = step * combs + i
            beam = beam_ref[:, comb_row].reshape(low, 2 * samples)
            wide = beam.astype(F32)
            power_ref[...] += jnp.sum((wide * wide).reshape(low // 8, 8, 2 * samples), 0)
            spectrum = jnp.dot(beam, time_ref[...], preferred_element_type=F32)
            turned = cmul(
                (turn_a_ref[0], turn_a_ref[1]),
                (turn_b_ref[0, pl.ds(comb_row, 1), :], turn_b_ref[1, pl.ds(comb_row, 1), :]),
            )
            halves = []
            for h in range(2):
                piece = spectrum[h * samples : (h + 1) * samples]
                moved = cmul((piece[:, :samples], piece[:, samples:]), turned)
                halves.append(jnp.concatenate(moved, 1).astype(BF16))
            moved = jnp.concatenate(halves, 0)
            mix_copy(comb_row).wait()
            mixed = jnp.dot(mix_ref[comb_row], moved, preferred_element_type=F32)
            grid_ref[comb_row, 0] = mixed[:low, :samples] - mixed[low:, samples:]
            grid_ref[comb_row, 1] = mixed[:low, samples:] + mixed[low:, :samples]

    @pl.when(step == first_steps)
    def _():
        mean_power = jnp.sum(power_ref[...]) / (samples * chans)
        factor = lax.rsqrt(jnp.full((1, samples), mean_power, F32) + EPSILON)
        for beta in range(2):
            for p in range(2):
                scaled_ref[beta, p] = after_ref[beta, p] * factor
        rate = 2 * rate_ref[0] + 1

        @pl.loop(0, low // 8)
        def _(tile):
            rows = pl.ds(pl.multiple_of(tile * 8, 8), 8)
            values = [(grid_ref[c, 0, rows, :], grid_ref[c, 1, rows, :]) for c in range(comb)]
            values = fft_list(values, 1)
            position = tile * 8 + lax.broadcasted_iota(jnp.int32, (8, samples), 0)
            wrapped = position < shift_ref[...]
            for m in range(comb):
                table = [
                    jnp.where(wrapped, before_ref[1, p, m : m + 1, :], before_ref[0, p, m : m + 1, :])
                    for p in range(2)
                ]
                values[m] = cmul(values[m], table)
            values = fft_list(values, -1)
            for k in range(comb):
                table = [
                    jnp.where(wrapped, scaled_ref[1, p, k : k + 1, :], scaled_ref[0, p, k : k + 1, :])
                    for p in range(2)
                ]
                real, imag = cmul(values[k], table)
                place = lax.rem(rate * k, comb)
                grid_ref[place, 0, rows, :] = real
                grid_ref[place, 1, rows, :] = imag

    @pl.when(step >= first_steps)
    def _():
        per = out_ref.shape[3] // low
        for i in range(per):
            high = (step - first_steps) * per + i
            both = jnp.concatenate([grid_ref[high, 0], grid_ref[high, 1]], 1).astype(BF16)
            result = lax.dot_general(
                time_ref[...], both, (((1,), (1,)), ((), ())), preferred_element_type=F32
            )
            out_ref[0, 0, :, i * low : (i + 1) * low] = result[:samples]
            out_ref[0, 1, :, i * low : (i + 1) * low] = result[samples:]


def dedisperse(beam, trial, samples, chans):
    low, comb = 2 * samples, chans // (2 * samples)
    tables = chirp_tables(2 * trial[0] + 1, samples, chans)
    time_mat = time_matrix(samples)
    mix = mix_matrices(samples, chans)
    first_steps, last_steps = comb // 2, 4
    vmem = pl.BlockSpec(memory_space=pltpu.VMEM)
    return pl.pallas_call(
        functools.partial(dedisperse_kernel, chans, first_steps),
        out_shape=jax.ShapeDtypeStruct((1, 2, samples, chans), F32),
        grid=(first_steps + last_steps,),
        in_specs=[pl.BlockSpec(memory_space=pltpu.SMEM), vmem, vmem, pl.BlockSpec(memory_space=pl.ANY)]
        + [vmem] * len(tables),
        out_specs=pl.BlockSpec(
            (1, 2, samples, chans // last_steps),
            lambda i: (0, 0, 0, jnp.maximum(i - first_steps, 0)),
        ),
        scratch_shapes=[
            pltpu.VMEM((comb, 2, low, samples), F32),
            pltpu.VMEM((8, 2 * samples), F32),
            pltpu.VMEM((2, 2, comb, samples), F32),
            pltpu.VMEM(mix.shape, BF16),
            pltpu.SemaphoreType.DMA((comb,)),
        ],
        compiler_params=pltpu.CompilerParams(vmem_limit_bytes=50 * 2**20),
        name="dedisperse",
    )(trial, beam, time_mat, mix, *tables)


def on_device(chan_devs, voltages, delays, pointing, dm_index, dish_mask):
    chan_dev, _, _, samples = voltages.shape
    chans = chan_dev * chan_devs
    comb = chans // (2 * samples)
    beam_dev = dm_index.shape[0]
    formed = form_beams(voltages, delays, pointing, dish_mask, chans, comb)
    formed = lax.all_to_all(formed, "chan", split_axis=0, concat_axis=0, tiled=True)
    part_rows = chan_dev // comb
    formed = formed.reshape(chan_devs, beam_dev, comb, part_rows, 2 * samples)
    if part_rows % 16:
        formed = jnp.transpose(formed, (1, 2, 0, 3, 4)).reshape(
            1, beam_dev, comb, chans // comb, 2 * samples
        )
    pieces = [
        dedisperse(formed[:, b], dm_index[b : b + 1], samples, chans) for b in range(beam_dev)
    ]
    return pieces[0] if beam_dev == 1 else jnp.concatenate(pieces, 0)


def solution(mesh):
    return jax.shard_map(
        functools.partial(on_device, mesh.shape["chan"]),
        mesh=mesh,
        in_specs=(
            P(("grp", "chan"), None, None, None),
            P(),
            P("grp"),
            P(("grp", "chan")),
            P("grp"),
        ),
        out_specs=P(("grp", "chan"), None, None, None),
        check_vma=False,
    )
```

```python
import functools
import math

import jax
import jax.numpy as jnp
from jax import lax
from jax.experimental import pallas as pl
from jax.experimental.pallas import tpu as pltpu
from jax.sharding import PartitionSpec as P

TWO_PI = 2.0 * math.pi
BAND_LOW = 0.856
BAND_WIDTH = 0.856
EPSILON = 1e-06
F32 = jnp.float32
BF16 = jnp.bfloat16


def cmul(a, b):
    return (a[0] * b[0] - a[1] * b[1], a[0] * b[1] + a[1] * b[0])


def cadd(a, b):
    return (a[0] + b[0], a[1] + b[1])


def csub(a, b):
    return (a[0] - b[0], a[1] - b[1])


def turn(a, num, den):
    num = num % den
    if num == 0:
        return a
    if 2 * num == den:
        return (-a[0], -a[1])
    if 4 * num == den:
        return (-a[1], a[0])
    if 4 * num == 3 * den:
        return (a[1], -a[0])
    if 8 * num % den == 0:
        root = math.sqrt(0.5)
        plus, minus = (a[0] + a[1]) * root, (a[0] - a[1]) * root
        return {1: (minus, plus), 3: (-plus, minus), 5: (-minus, -plus), 7: (plus, -minus)}[
            8 * num // den
        ]
    cosine, sine = math.cos(TWO_PI * num / den), math.sin(TWO_PI * num / den)
    return (a[0] * cosine - a[1] * sine, a[0] * sine + a[1] * cosine)


def fft_list(values, sign):
    points = len(values)
    if points == 1:
        return values
    if points == 2:
        return [cadd(values[0], values[1]), csub(values[0], values[1])]
    quarter = points // 4
    parts = [fft_list(values[i::4], sign) for i in range(4)]
    out = [None] * points
    for k in range(quarter):
        a, b, c, d = [turn(parts[i][k], sign * i * k, points) for i in range(4)]
        s0, s1 = cadd(a, c), csub(a, c)
        s2, s3 = cadd(b, d), turn(csub(b, d), sign, 4)
        out[k] = cadd(s0, s2)
        out[k + quarter] = cadd(s1, s3)
        out[k + 2 * quarter] = csub(s0, s2)
        out[k + 3 * quarter] = csub(s1, s3)
    return out


def small_phasor(x):
    y = x * x
    cosine = 1.0 - y * (1 / 2 - y * (1 / 24 - y * (1 / 720)))
    return cosine, x * (1.0 - y * (1 / 6 - y * (1 / 120 - y * (1 / 5040))))


def wide_phasor(x):
    quarter = jnp.floor(x * (2.0 / math.pi) + 0.5)
    rest = x - quarter * 1.5703125
    rest = rest - quarter * 4.837512969970703125e-4
    rest = rest - quarter * 7.54978995489188e-8
    y = rest * rest
    cosine = 1.0 - y * (0.5 - y * (1 / 24 - y * (1 / 720 - y * (1 / 40320))))
    sine = rest * (1.0 - y * (1 / 6 - y * (1 / 120 - y * (1 / 5040 - y * (1 / 362880)))))
    turns = quarter.astype(jnp.int32)
    swap = (turns & 1) == 1
    even, odd = jnp.where(swap, sine, cosine), jnp.where(swap, cosine, sine)
    return (
        jnp.where(((turns + 1) & 2) == 2, -even, even),
        jnp.where((turns & 2) == 2, -odd, odd),
    )


def beam_kernel(
    chans, comb, point_ref, delay_hbm, mask_hbm, volt_hbm, out_hbm,
    delay_ref, mask_ref, volt_ref, out_ref, zero_ref, fine_ref, coarse_ref, rows_ref,
    small_sem, volt_sem, out_sem,
):
    part_rows = volt_ref.shape[0]
    beams = out_ref.shape[0]
    dishes = delay_ref.shape[0]
    samples = rows_ref.shape[3]
    chan_dev = part_rows * comb
    group = rows_ref.shape[2] // beams
    group_combs = group // part_rows
    groups = chan_dev // group
    chunks = volt_sem.shape[0]
    per = groups // chunks

    def volt_copy(g):
        combs = pl.ds(g * per * group_combs, per * group_combs)
        return pltpu.make_async_copy(volt_hbm.at[:, combs], volt_ref.at[:, combs], volt_sem.at[g])

    def out_copy(g):
        rows = pl.ds(g * per * group, per * group)
        return pltpu.make_async_copy(out_ref.at[:, rows], out_hbm.at[:, rows], out_sem.at[g])

    delay_copy = pltpu.make_async_copy(delay_hbm, delay_ref, small_sem.at[0])
    mask_copy = pltpu.make_async_copy(mask_hbm, mask_ref, small_sem.at[1])
    delay_copy.start()
    mask_copy.start()
    for g in range(chunks):
        volt_copy(g).start()
    delay_copy.wait()
    mask_copy.wait()

    table_rows = delay_ref.shape[1]
    place = lax.broadcasted_iota(jnp.int32, (beams, table_rows), 1)
    which = lax.broadcasted_iota(jnp.int32, (beams, table_rows), 0)
    wanted = jnp.zeros((beams, table_rows), jnp.int32)
    for b in range(beams):
        wanted = jnp.where(which == b, point_ref[b], wanted)
    select = (wanted == place).astype(F32).astype(BF16)
    rest, pieces = delay_ref[...], []
    for _ in range(3):
        piece = rest.astype(BF16)
        rest = rest - piece.astype(F32)
        pieces += [piece, piece]
    found = lax.dot_general(
        select,
        jnp.concatenate(pieces, 0),
        (((1,), (1,)), ((), ())),
        preferred_element_type=F32,
    )
    width = 2 * dishes
    tau = (found[:, 2 * width :] + found[:, width : 2 * width]) + found[:, :width]
    first = lax.axis_index("chan") * chan_dev
    frequency = BAND_LOW + BAND_WIDTH * (first.astype(F32) + 0.5) / chans
    angle = (TWO_PI * frequency) * tau
    gain_half = mask_ref[...].astype(F32) / math.sqrt(dishes)
    gain = jnp.concatenate([gain_half, gain_half], 1)
    cosine, sine = wide_phasor(angle)
    cosine, sine = cosine * gain, sine * gain
    left = lax.broadcasted_iota(jnp.int32, (beams, 2 * dishes), 1) < dishes
    zero_ref[0] = jnp.where(left, cosine, sine)
    zero_ref[1] = jnp.where(left, -sine, cosine)
    for table_ref, stride in ((fine_ref, 1), (coarse_ref, comb)):
        shift = (TWO_PI * BAND_WIDTH / chans * stride) * tau
        count = table_ref.shape[0]
        cosine, sine = small_phasor(shift)
        powers = [(jnp.ones_like(tau), jnp.zeros_like(tau)), (cosine, -sine)]
        for k in range(2, count):
            powers.append(cmul(powers[k // 2], powers[k - k // 2]))
        for k in range(count):
            table_ref[k, 0] = powers[k][0]
            table_ref[k, 1] = powers[k][1]

    for g in range(groups):
        if g % per == 0:
            volt_copy(g // per).wait()
        slot = g % rows_ref.shape[0]
        for i in range(group):
            ja, cb = i % part_rows, g * group_combs + i // part_rows
            if ja == 0:
                base = cmul((zero_ref[0], zero_ref[1]), (fine_ref[cb, 0], fine_ref[cb, 1]))
            weight = cmul(base, (coarse_ref[ja, 0], coarse_ref[ja, 1]))
            stacked = jnp.concatenate(weight, 0).astype(BF16)
            formed = jnp.dot(stacked, volt_ref[ja, cb], preferred_element_type=F32)
            rows_ref[slot, 0, pl.ds(i, beams, stride=group), :] = formed[:beams]
            rows_ref[slot, 1, pl.ds(i, beams, stride=group), :] = formed[beams:]
        rows = pl.ds(g * group, group)
        for p in range(2):
            out_ref[:, rows, p * samples : (p + 1) * samples] = (
                rows_ref[slot, p].reshape(beams, group, samples).astype(BF16)
            )
        if g % per == per - 1:
            out_copy(g // per).start()

    for g in range(chunks):
        out_copy(g).wait()


def form_beams(voltages, delays, pointing, dish_mask, chans, comb):
    chan_dev, _, dishes, samples = voltages.shape
    beams = pointing.shape[0]
    part_rows = chan_dev // comb
    group = part_rows * max(1, 16 // part_rows)
    chunks = math.gcd(2, chan_dev // group)
    hbm = pl.BlockSpec(memory_space=pltpu.HBM)
    volt = voltages.reshape(part_rows, comb, 2 * dishes, samples)
    return pl.pallas_call(
        functools.partial(beam_kernel, chans, comb),
        out_shape=jax.ShapeDtypeStruct((beams, chan_dev, 2 * samples), BF16),
        in_specs=[pl.BlockSpec(memory_space=pltpu.SMEM), hbm, hbm, hbm],
        out_specs=hbm,
        scratch_shapes=[
            pltpu.VMEM((dishes, delays.shape[0]), F32),
            pltpu.VMEM((1, dishes), jnp.int32),
            pltpu.VMEM(volt.shape, BF16),
            pltpu.VMEM((beams, chan_dev, 2 * samples), BF16),
            pltpu.VMEM((2, beams, 2 * dishes), F32),
            pltpu.VMEM((comb, 2, beams, 2 * dishes), F32),
            pltpu.VMEM((part_rows, 2, beams, 2 * dishes), F32),
            pltpu.VMEM((2, 2, beams * group, samples), F32),
            pltpu.SemaphoreType.DMA((2,)),
            pltpu.SemaphoreType.DMA((chunks,)),
            pltpu.SemaphoreType.DMA((chunks,)),
        ],
        compiler_params=pltpu.CompilerParams(vmem_limit_bytes=60 * 2**20),
        name="form_beams",
    )(pointing, delays.T, dish_mask.reshape(1, dishes), volt)


def phasor(phase, points):
    half = points // 2
    angle = (TWO_PI / points) * ((phase + half) % points - half).astype(F32)
    return jnp.stack([jnp.cos(angle), jnp.sin(angle)], 0)


def chirp_tables(rate, samples, chans):
    length = samples * chans
    low, comb = 2 * samples, chans // (2 * samples)
    f = jnp.arange(samples, dtype=jnp.int32)[None, :]
    shift = 2 * rate * f % chans
    shift_low, shift_high = shift % low, shift // low
    inverse = rate * (2 - rate * rate) % (2 * comb)
    m = jnp.arange(comb, dtype=jnp.int32)[:, None]
    unit = length // (2 * comb)
    c_a = jnp.arange(samples, dtype=jnp.int32)[:, None]
    turn_a = phasor(-(rate * c_a * f % samples), samples)
    turn_b = phasor(-(rate * m * f % (chans // 2)), chans // 2)
    quad = inverse * m * m % (2 * comb) * unit
    place = (m - shift_high) % comb
    wrap = jnp.where(place == 0, comb, 0)
    before = [phasor(quad - (place + beta * wrap) * low * f, length) for beta in range(2)]
    place = rate * m % comb
    quad = inverse * place * place % (2 * comb) * unit
    gauss_phase = -(rate * m * m % (2 * comb)) * unit
    gauss = jnp.sum(phasor(gauss_phase, length), axis=1)
    scale = 2 * samples / (length * math.sqrt(chans))
    turned = phasor(quad + low * place * f + f * shift_low - rate * f * f % length, length)
    after = cmul((turned[0], turned[1]), (gauss[0] * scale, gauss[1] * scale))
    return turn_a, turn_b, jnp.stack(before), jnp.stack(after), shift_low


def time_matrix(samples):
    t = jnp.arange(samples, dtype=jnp.int32)
    cosine, sine = phasor(t[:, None] * t[None, :] % samples, samples)
    return jnp.concatenate(
        [jnp.concatenate([cosine, -sine], 1), jnp.concatenate([sine, cosine], 1)], 0
    ).astype(BF16)


def mix_matrices(samples, chans):
    low, comb = 2 * samples, chans // (2 * samples)
    n = jnp.arange(low, dtype=jnp.int32)
    c_b = jnp.arange(comb, dtype=jnp.int32)
    product = (comb * n[None, None, :] + c_b[:, None, None]) * n[None, :, None] % chans
    cosine, sine = phasor(product, chans)
    both = jnp.stack([cosine.reshape(comb, low // 8, 8, low), sine.reshape(comb, low // 8, 8, low)], 2)
    return both.reshape(comb, 2 * low, low).astype(BF16)


def dedisperse_kernel(
    chans, rate_ref, beam_ref, time_ref, mix_hbm, turn_a_ref, turn_b_ref, before_ref, after_ref,
    shift_ref, out_hbm, grid_ref, power_ref, scaled_ref, mix_ref, out_ref, moved_ref, mix_sem, out_sem,
):
    samples = turn_a_ref.shape[1]
    low, comb = 2 * samples, grid_ref.shape[0]
    ahead = min(16, comb)

    def mix_copy(c):
        part = pl.ds(c * (comb // 2), comb // 2)
        return pltpu.make_async_copy(mix_hbm.at[part], mix_ref.at[part], mix_sem.at[c])

    def out_copy(high):
        lanes = pl.ds(high * low, low)
        return pltpu.make_async_copy(
            out_ref.at[:, :, lanes], out_hbm.at[0, :, :, lanes], out_sem.at[high]
        )

    for c in range(2):
        mix_copy(c).start()
    power_ref[...] = jnp.zeros_like(power_ref)

    for c_b in range(comb):
        beam = beam_ref[:, c_b].reshape(low, 2 * samples)
        wide = beam.astype(F32)
        power_ref[...] += jnp.sum((wide * wide).reshape(low // 8, 8, 2 * samples), 0)
        spectrum = jnp.dot(beam, time_ref[...], preferred_element_type=F32)
        turned = cmul(
            (turn_a_ref[0], turn_a_ref[1]),
            (turn_b_ref[0, pl.ds(c_b, 1), :], turn_b_ref[1, pl.ds(c_b, 1), :]),
        )
        halves = []
        for h in range(2):
            piece = spectrum[h * samples : (h + 1) * samples]
            moved = cmul((piece[:, :samples], piece[:, samples:]), turned)
            halves.append(jnp.concatenate(moved, 1).astype(BF16))
        moved_ref[c_b] = jnp.concatenate(halves, 0)

    for c_b in range(comb):
        moved = moved_ref[c_b]
        if c_b % (comb // 2) == 0:
            mix_copy(c_b // (comb // 2)).wait()


        mixed = jnp.dot(mix_ref[c_b], moved, preferred_element_type=F32)
        mixed = mixed.reshape(low // 8, 2, 8, 2 * samples)
        real = mixed[:, 0, :, :samples] - mixed[:, 1, :, samples:]
        imag = mixed[:, 0, :, samples:] + mixed[:, 1, :, :samples]
        grid_ref[c_b, 0] = real.reshape(low, samples)
        grid_ref[c_b, 1] = imag.reshape(low, samples)

    mean_power = jnp.sum(power_ref[...]) / (samples * chans)
    factor = lax.rsqrt(jnp.full((1, samples), mean_power, F32) + EPSILON)
    for p in range(2):
        scaled_ref[p] = after_ref[p] * factor
    rate = 2 * rate_ref[0] + 1

    @pl.loop(0, low // 8, unroll=1)
    def _(tile):
        rows = pl.ds(pl.multiple_of(tile * 8, 8), 8)
        values = [(grid_ref[c, 0, rows, :], grid_ref[c, 1, rows, :]) for c in range(comb)]
        values = fft_list(values, 1)
        position = tile * 8 + lax.broadcasted_iota(jnp.int32, (8, samples), 0)
        wrapped = position < shift_ref[...]
        for m in range(comb):
            table = [
                jnp.where(wrapped, before_ref[1, p, m : m + 1, :], before_ref[0, p, m : m + 1, :])
                for p in range(2)
            ]
            values[m] = cmul(values[m], table)
        values = fft_list(values, -1)
        for k in range(comb):
            real, imag = cmul(values[k], [scaled_ref[p, k : k + 1, :] for p in range(2)])
            place = lax.rem(rate * k, comb)
            grid_ref[place, 0, rows, :] = real
            grid_ref[place, 1, rows, :] = imag

    @pl.loop(0, comb, unroll=4)
    def _(high):
        both = jnp.concatenate([grid_ref[high, 0], grid_ref[high, 1]], 1).astype(BF16)
        result = lax.dot_general(
            time_ref[...], both, (((1,), (1,)), ((), ())), preferred_element_type=F32
        )
        lanes = pl.ds(pl.multiple_of(high * low, low), low)
        out_ref[0, :, lanes] = result[:samples]
        out_ref[1, :, lanes] = result[samples:]
        out_copy(high).start()

    @pl.loop(0, comb)
    def _(high):
        out_copy(high).wait()


def dedisperse(beam, trial, samples, chans):
    low, comb = 2 * samples, chans // (2 * samples)
    tables = chirp_tables(2 * trial[0] + 1, samples, chans)
    time_mat = time_matrix(samples)
    mix = mix_matrices(samples, chans)
    hbm = pl.BlockSpec(memory_space=pltpu.HBM)
    vmem = pl.BlockSpec(memory_space=pltpu.VMEM)
    return pl.pallas_call(
        functools.partial(dedisperse_kernel, chans),
        out_shape=jax.ShapeDtypeStruct((1, 2, samples, chans), F32),
        in_specs=[pl.BlockSpec(memory_space=pltpu.SMEM), vmem, vmem, hbm] + [vmem] * len(tables),
        out_specs=hbm,
        scratch_shapes=[
            pltpu.VMEM((comb, 2, low, samples), F32),
            pltpu.VMEM((8, 2 * samples), F32),
            pltpu.VMEM((2, comb, samples), F32),
            pltpu.VMEM(mix.shape, BF16),
            pltpu.VMEM((2, samples, chans), F32),
            pltpu.VMEM((comb, low, low), BF16),
            pltpu.SemaphoreType.DMA((comb,)),
            pltpu.SemaphoreType.DMA((comb,)),
        ],
        compiler_params=pltpu.CompilerParams(vmem_limit_bytes=50 * 2**20),
        name="dedisperse",
    )(trial, beam, time_mat, mix, *tables)


def on_device(chan_devs, voltages, delays, pointing, dm_index, dish_mask):
    chan_dev, _, _, samples = voltages.shape
    chans = chan_dev * chan_devs
    comb = chans // (2 * samples)
    beam_dev = dm_index.shape[0]
    formed = form_beams(voltages, delays, pointing, dish_mask, chans, comb)
    formed = lax.all_to_all(formed, "chan", split_axis=0, concat_axis=0, tiled=True)
    part_rows = chan_dev // comb
    formed = formed.reshape(chan_devs, beam_dev, comb, part_rows, 2 * samples)
    if part_rows % 16:
        formed = jnp.transpose(formed, (1, 2, 0, 3, 4)).reshape(
            1, beam_dev, comb, chans // comb, 2 * samples
        )
    pieces = [
        dedisperse(formed[:, b], dm_index[b : b + 1], samples, chans) for b in range(beam_dev)
    ]
    return pieces[0] if beam_dev == 1 else jnp.concatenate(pieces, 0)


def solution(mesh):
    return jax.shard_map(
        functools.partial(on_device, mesh.shape["chan"]),
        mesh=mesh,
        in_specs=(
            P(("grp", "chan"), None, None, None),
            P(),
            P("grp"),
            P(("grp", "chan")),
            P("grp"),
        ),
        out_specs=P(("grp", "chan"), None, None, None),
        check_vma=False,
    )
```

```python
import functools
import math

import jax
import jax.numpy as jnp
from jax import lax
from jax.experimental import pallas as pl
from jax.experimental.pallas import tpu as pltpu
from jax.sharding import PartitionSpec as P

TWO_PI = 2.0 * math.pi
BAND_LOW = 0.856
BAND_WIDTH = 0.856
EPSILON = 1e-06
F32 = jnp.float32
BF16 = jnp.bfloat16


def cmul(a, b):
    return (a[0] * b[0] - a[1] * b[1], a[0] * b[1] + a[1] * b[0])


def cadd(a, b):
    return (a[0] + b[0], a[1] + b[1])


def csub(a, b):
    return (a[0] - b[0], a[1] - b[1])


def turn(a, num, den):
    num = num % den
    if num == 0:
        return a
    if 2 * num == den:
        return (-a[0], -a[1])
    if 4 * num == den:
        return (-a[1], a[0])
    if 4 * num == 3 * den:
        return (a[1], -a[0])
    if 8 * num % den == 0:
        root = math.sqrt(0.5)
        plus, minus = (a[0] + a[1]) * root, (a[0] - a[1]) * root
        return {1: (minus, plus), 3: (-plus, minus), 5: (-minus, -plus), 7: (plus, -minus)}[
            8 * num // den
        ]
    cosine, sine = math.cos(TWO_PI * num / den), math.sin(TWO_PI * num / den)
    return (a[0] * cosine - a[1] * sine, a[0] * sine + a[1] * cosine)


def fft_list(values, sign):
    points = len(values)
    if points == 1:
        return values
    if points == 2:
        return [cadd(values[0], values[1]), csub(values[0], values[1])]
    quarter = points // 4
    parts = [fft_list(values[i::4], sign) for i in range(4)]
    out = [None] * points
    for k in range(quarter):
        a, b, c, d = [turn(parts[i][k], sign * i * k, points) for i in range(4)]
        s0, s1 = cadd(a, c), csub(a, c)
        s2, s3 = cadd(b, d), turn(csub(b, d), sign, 4)
        out[k] = cadd(s0, s2)
        out[k + quarter] = cadd(s1, s3)
        out[k + 2 * quarter] = csub(s0, s2)
        out[k + 3 * quarter] = csub(s1, s3)
    return out


def small_phasor(x):
    y = x * x
    cosine = 1.0 - y * (1 / 2 - y * (1 / 24 - y * (1 / 720)))
    return cosine, x * (1.0 - y * (1 / 6 - y * (1 / 120 - y * (1 / 5040))))


def wide_phasor(x):
    quarter = jnp.floor(x * (2.0 / math.pi) + 0.5)
    rest = x - quarter * 1.5703125
    rest = rest - quarter * 4.837512969970703125e-4
    rest = rest - quarter * 7.54978995489188e-8
    y = rest * rest
    cosine = 1.0 - y * (0.5 - y * (1 / 24 - y * (1 / 720 - y * (1 / 40320))))
    sine = rest * (1.0 - y * (1 / 6 - y * (1 / 120 - y * (1 / 5040 - y * (1 / 362880)))))
    turns = quarter.astype(jnp.int32)
    swap = (turns & 1) == 1
    even, odd = jnp.where(swap, sine, cosine), jnp.where(swap, cosine, sine)
    return (
        jnp.where(((turns + 1) & 2) == 2, -even, even),
        jnp.where((turns & 2) == 2, -odd, odd),
    )


def beam_kernel(
    chans, comb, point_ref, delay_hbm, mask_hbm, volt_hbm, out_hbm,
    delay_ref, mask_ref, volt_ref, out_ref, zero_ref, fine_ref, coarse_ref, rows_ref,
    small_sem, volt_sem, out_sem,
):
    part_rows = volt_ref.shape[0]
    beams = out_ref.shape[0]
    dishes = delay_ref.shape[0]
    samples = rows_ref.shape[3]
    chan_dev = part_rows * comb
    group = rows_ref.shape[2] // beams
    group_combs = group // part_rows
    groups = chan_dev // group
    chunks = volt_sem.shape[0]
    ends = [groups * end // 16 for end in (6, 11, 14, 16)] if chunks > 1 else [groups]
    begins = [0] + ends[:-1]

    def volt_copy(g):
        combs = pl.ds(begins[g] * group_combs, (ends[g] - begins[g]) * group_combs)
        return pltpu.make_async_copy(volt_hbm.at[:, combs], volt_ref.at[:, combs], volt_sem.at[g])

    def out_copy(g):
        rows = pl.ds(begins[g] * group, (ends[g] - begins[g]) * group)
        return pltpu.make_async_copy(out_ref.at[:, rows], out_hbm.at[:, rows], out_sem.at[g])

    delay_copy = pltpu.make_async_copy(delay_hbm, delay_ref, small_sem.at[0])
    mask_copy = pltpu.make_async_copy(mask_hbm, mask_ref, small_sem.at[1])
    delay_copy.start()
    mask_copy.start()
    volt_copy(0).start()
    delay_copy.wait()
    mask_copy.wait()
    if chunks > 1:
        volt_copy(1).start()

    table_rows = delay_ref.shape[1]
    place = lax.broadcasted_iota(jnp.int32, (beams, table_rows), 1)
    which = lax.broadcasted_iota(jnp.int32, (beams, table_rows), 0)
    wanted = jnp.zeros((beams, table_rows), jnp.int32)
    for b in range(beams):
        wanted = jnp.where(which == b, point_ref[b], wanted)
    select = (wanted == place).astype(F32).astype(BF16)
    rest, pieces = delay_ref[...], []
    for _ in range(3):
        piece = rest.astype(BF16)
        rest = rest - piece.astype(F32)
        pieces += [piece, piece]
    found = lax.dot_general(
        select,
        jnp.concatenate(pieces, 0),
        (((1,), (1,)), ((), ())),
        preferred_element_type=F32,
    )
    width = 2 * dishes
    tau = (found[:, 2 * width :] + found[:, width : 2 * width]) + found[:, :width]
    first = lax.axis_index("chan") * chan_dev
    frequency = BAND_LOW + BAND_WIDTH * (first.astype(F32) + 0.5) / chans
    angle = (TWO_PI * frequency) * tau
    gain_half = mask_ref[...].astype(F32) / math.sqrt(dishes)
    gain = jnp.concatenate([gain_half, gain_half], 1)
    cosine, sine = wide_phasor(angle)
    cosine, sine = cosine * gain, sine * gain
    left = lax.broadcasted_iota(jnp.int32, (beams, 2 * dishes), 1) < dishes
    zero_ref[0] = jnp.where(left, cosine, sine)
    zero_ref[1] = jnp.where(left, -sine, cosine)
    for table_ref, stride in ((fine_ref, 1), (coarse_ref, comb)):
        shift = (TWO_PI * BAND_WIDTH / chans * stride) * tau
        count = table_ref.shape[0]
        cosine, sine = small_phasor(shift)
        powers = [(jnp.ones_like(tau), jnp.zeros_like(tau)), (cosine, -sine)]
        for k in range(2, count):
            powers.append(cmul(powers[k // 2], powers[k - k // 2]))
        for k in range(count):
            table_ref[k, 0] = powers[k][0]
            table_ref[k, 1] = powers[k][1]

    for g in range(groups):
        if g in begins:
            chunk = begins.index(g)
            volt_copy(chunk).wait()
            if chunk + 2 < chunks:
                volt_copy(chunk + 2).start()
        slot = g % rows_ref.shape[0]
        for i in range(0, group, 2):
            weights, sources = [], []
            for k in range(i, i + 2):
                ja, cb = k % part_rows, g * group_combs + k // part_rows
                if ja == 0:
                    base = cmul((zero_ref[0], zero_ref[1]), (fine_ref[cb, 0], fine_ref[cb, 1]))
                weight = cmul(base, (coarse_ref[ja, 0], coarse_ref[ja, 1]))
                weights.append(jnp.concatenate(weight, 0).astype(BF16))
                sources.append(volt_ref[ja, cb])
            blank = jnp.zeros_like(weights[0])
            stacked = jnp.concatenate(
                [jnp.concatenate([weights[0], blank], 1), jnp.concatenate([blank, weights[1]], 1)], 0
            )
            formed = jnp.dot(stacked, jnp.concatenate(sources, 0), preferred_element_type=F32)
            for k in range(2):
                for p in range(2):
                    rows_ref[slot, p, pl.ds(i + k, beams, stride=group), :] = formed[
                        (2 * k + p) * beams : (2 * k + p + 1) * beams
                    ]
        rows = pl.ds(g * group, group)
        for p in range(2):
            out_ref[:, rows, p * samples : (p + 1) * samples] = (
                rows_ref[slot, p].reshape(beams, group, samples).astype(BF16)
            )
        if g + 1 in ends:
            out_copy(chunk).start()

    for g in range(chunks):
        out_copy(g).wait()


def form_beams(voltages, delays, pointing, dish_mask, chans, comb):
    chan_dev, _, dishes, samples = voltages.shape
    beams = pointing.shape[0]
    part_rows = chan_dev // comb
    group = part_rows * max(1, 16 // part_rows)
    chunks = 4 if (chan_dev // group) % 16 == 0 else 1
    hbm = pl.BlockSpec(memory_space=pltpu.HBM)
    volt = voltages.reshape(part_rows, comb, 2 * dishes, samples)
    return pl.pallas_call(
        functools.partial(beam_kernel, chans, comb),
        out_shape=jax.ShapeDtypeStruct((beams, chan_dev, 2 * samples), BF16),
        in_specs=[pl.BlockSpec(memory_space=pltpu.SMEM), hbm, hbm, hbm],
        out_specs=hbm,
        scratch_shapes=[
            pltpu.VMEM((dishes, delays.shape[0]), F32),
            pltpu.VMEM((1, dishes), jnp.int32),
            pltpu.VMEM(volt.shape, BF16),
            pltpu.VMEM((beams, chan_dev, 2 * samples), BF16),
            pltpu.VMEM((2, beams, 2 * dishes), F32),
            pltpu.VMEM((comb, 2, beams, 2 * dishes), F32),
            pltpu.VMEM((part_rows, 2, beams, 2 * dishes), F32),
            pltpu.VMEM((2, 2, beams * group, samples), F32),
            pltpu.SemaphoreType.DMA((2,)),
            pltpu.SemaphoreType.DMA((chunks,)),
            pltpu.SemaphoreType.DMA((chunks,)),
        ],
        compiler_params=pltpu.CompilerParams(vmem_limit_bytes=60 * 2**20),
        name="form_beams",
    )(pointing, delays.T, dish_mask.reshape(1, dishes), volt)


def phasor(phase, points):
    half = points // 2
    angle = (TWO_PI / points) * ((phase + half) % points - half).astype(F32)
    return jnp.stack([jnp.cos(angle), jnp.sin(angle)], 0)


def chirp_tables(rate, samples, chans):
    length = samples * chans
    low, comb = 2 * samples, chans // (2 * samples)
    f = jnp.arange(samples, dtype=jnp.int32)[None, :]
    shift = 2 * rate * f % chans
    shift_low, shift_high = shift % low, shift // low
    inverse = rate * (2 - rate * rate) % (2 * comb)
    m = jnp.arange(comb, dtype=jnp.int32)[:, None]
    unit = length // (2 * comb)
    c_a = jnp.arange(samples, dtype=jnp.int32)[:, None]
    turn_a = phasor(-(rate * c_a * f % samples), samples)
    turn_b = phasor(-(rate * m * f % (chans // 2)), chans // 2)
    quad = inverse * m * m % (2 * comb) * unit
    place = (m - shift_high) % comb
    wrap = jnp.where(place == 0, comb, 0)
    before = [phasor(quad - (place + beta * wrap) * low * f, length) for beta in range(2)]
    place = rate * m % comb
    quad = inverse * place * place % (2 * comb) * unit
    gauss_phase = -(rate * m * m % (2 * comb)) * unit
    gauss = jnp.sum(phasor(gauss_phase, length), axis=1)
    scale = 2 * samples / (length * math.sqrt(chans))
    turned = phasor(quad + low * place * f + f * shift_low - rate * f * f % length, length)
    after = cmul((turned[0], turned[1]), (gauss[0] * scale, gauss[1] * scale))
    return turn_a, turn_b, jnp.stack(before), jnp.stack(after), shift_low


def time_matrix(samples):
    t = jnp.arange(samples, dtype=jnp.int32)
    cosine, sine = phasor(t[:, None] * t[None, :] % samples, samples)
    return jnp.concatenate(
        [jnp.concatenate([cosine, -sine], 1), jnp.concatenate([sine, cosine], 1)], 0
    ).astype(BF16)


def mix_matrices(samples, chans):
    low, comb = 2 * samples, chans // (2 * samples)
    n = jnp.arange(low, dtype=jnp.int32)
    c_b = jnp.arange(comb, dtype=jnp.int32)
    product = (comb * n[None, None, :] + c_b[:, None, None]) * n[None, :, None] % chans
    cosine, sine = phasor(product, chans)
    both = jnp.stack([cosine.reshape(comb, low // 8, 8, low), sine.reshape(comb, low // 8, 8, low)], 2)
    return both.reshape(comb, 2 * low, low).astype(BF16)


def dedisperse_kernel(
    chans, rate_ref, beam_ref, time_ref, mix_hbm, turn_a_ref, turn_b_ref, before_ref, after_ref,
    shift_ref, out_hbm, grid_ref, power_ref, scaled_ref, mix_ref, out_ref, moved_ref, mix_sem, out_sem,
):
    samples = turn_a_ref.shape[1]
    low, comb = 2 * samples, grid_ref.shape[0]

    def mix_copy(c):
        part = pl.ds(c * (comb // 2), comb // 2)
        return pltpu.make_async_copy(mix_hbm.at[part], mix_ref.at[part], mix_sem.at[c])

    def out_copy(half, high):
        lanes = pl.ds(high * low + half * samples, samples)
        return pltpu.make_async_copy(
            out_ref.at[:, :, lanes], out_hbm.at[0, :, :, lanes], out_sem.at[half, high]
        )

    for c in range(2):
        mix_copy(c).start()
    power_ref[...] = jnp.zeros_like(power_ref)

    for c_b in range(comb):
        beam = beam_ref[:, c_b].reshape(low, 2 * samples)
        wide = beam.astype(F32)
        power_ref[...] += jnp.sum((wide * wide).reshape(low // 8, 8, 2 * samples), 0)
        spectrum = jnp.dot(beam, time_ref[...], preferred_element_type=F32)
        turned = cmul(
            (turn_a_ref[0], turn_a_ref[1]),
            (turn_b_ref[0, pl.ds(c_b, 1), :], turn_b_ref[1, pl.ds(c_b, 1), :]),
        )
        halves = []
        for h in range(2):
            piece = spectrum[h * samples : (h + 1) * samples]
            moved = cmul((piece[:, :samples], piece[:, samples:]), turned)
            halves.append(jnp.concatenate(moved, 1).astype(BF16))
        moved_ref[c_b] = jnp.concatenate(halves, 0)

    for c_b in range(comb):
        moved = moved_ref[c_b]
        if c_b % (comb // 2) == 0:
            mix_copy(c_b // (comb // 2)).wait()

        mixed = jnp.dot(mix_ref[c_b], moved, preferred_element_type=F32)
        mixed = mixed.reshape(low // 8, 2, 8, 2 * samples)
        real = mixed[:, 0, :, :samples] - mixed[:, 1, :, samples:]
        imag = mixed[:, 0, :, samples:] + mixed[:, 1, :, :samples]
        grid_ref[c_b, 0] = real.reshape(low, samples)
        grid_ref[c_b, 1] = imag.reshape(low, samples)

    mean_power = jnp.sum(power_ref[...]) / (samples * chans)
    factor = lax.rsqrt(jnp.full((1, samples), mean_power, F32) + EPSILON)
    for p in range(2):
        scaled_ref[p] = after_ref[p] * factor
    rate = 2 * rate_ref[0] + 1

    def spread(tile):
        rows = pl.ds(pl.multiple_of(tile * 8, 8), 8)
        values = [(grid_ref[c, 0, rows, :], grid_ref[c, 1, rows, :]) for c in range(comb)]
        values = fft_list(values, 1)
        position = tile * 8 + lax.broadcasted_iota(jnp.int32, (8, samples), 0)
        wrapped = position < shift_ref[...]
        for m in range(comb):
            table = [
                jnp.where(wrapped, before_ref[1, p, m : m + 1, :], before_ref[0, p, m : m + 1, :])
                for p in range(2)
            ]
            values[m] = cmul(values[m], table)
        values = fft_list(values, -1)
        for k in range(comb):
            real, imag = cmul(values[k], [scaled_ref[p, k : k + 1, :] for p in range(2)])
            place = lax.rem(rate * k, comb)
            grid_ref[place, 0, rows, :] = real
            grid_ref[place, 1, rows, :] = imag

    def finish(half, high):
        rows = pl.ds(half * samples, samples)
        both = [
            jnp.concatenate([grid_ref[high + i, 0, rows], grid_ref[high + i, 1, rows]], 1)
            for i in range(2)
        ]
        result = lax.dot_general(
            time_ref[...],
            jnp.concatenate(both, 0).astype(BF16),
            (((1,), (1,)), ((), ())),
            preferred_element_type=F32,
        )
        for i in range(2):
            lanes = pl.ds((high + i) * low + half * samples, samples)
            piece = result[:, i * samples : (i + 1) * samples]
            out_ref[0, :, lanes] = piece[:samples]
            out_ref[1, :, lanes] = piece[samples:]

    tiles = samples // 8
    for half in range(2):

        @pl.loop(0, tiles, unroll=1)
        def _(tile):
            spread(half * tiles + tile)

        for first in range(0, comb, 4):
            for high in range(first, first + 4, 2):
                finish(half, high)
            for high in range(first, first + 4):
                out_copy(half, high).start()

    for half in range(2):

        @pl.loop(0, comb)
        def _(high):
            out_copy(half, high).wait()


def dedisperse(beam, trial, samples, chans):
    low, comb = 2 * samples, chans // (2 * samples)
    tables = chirp_tables(2 * trial[0] + 1, samples, chans)
    time_mat = time_matrix(samples)
    mix = mix_matrices(samples, chans)
    hbm = pl.BlockSpec(memory_space=pltpu.HBM)
    vmem = pl.BlockSpec(memory_space=pltpu.VMEM)
    return pl.pallas_call(
        functools.partial(dedisperse_kernel, chans),
        out_shape=jax.ShapeDtypeStruct((1, 2, samples, chans), F32),
        in_specs=[pl.BlockSpec(memory_space=pltpu.SMEM), vmem, vmem, hbm] + [vmem] * len(tables),
        out_specs=hbm,
        scratch_shapes=[
            pltpu.VMEM((comb, 2, low, samples), F32),
            pltpu.VMEM((8, 2 * samples), F32),
            pltpu.VMEM((2, comb, samples), F32),
            pltpu.VMEM(mix.shape, BF16),
            pltpu.VMEM((2, samples, chans), F32),
            pltpu.VMEM((comb, low, low), BF16),
            pltpu.SemaphoreType.DMA((2,)),
            pltpu.SemaphoreType.DMA((2, comb)),
        ],
        compiler_params=pltpu.CompilerParams(vmem_limit_bytes=50 * 2**20),
        name="dedisperse",
    )(trial, beam, time_mat, mix, *tables)


def on_device(chan_devs, voltages, delays, pointing, dm_index, dish_mask):
    chan_dev, _, _, samples = voltages.shape
    chans = chan_dev * chan_devs
    comb = chans // (2 * samples)
    beam_dev = dm_index.shape[0]
    formed = form_beams(voltages, delays, pointing, dish_mask, chans, comb)
    formed = lax.all_to_all(formed, "chan", split_axis=0, concat_axis=0, tiled=True)
    part_rows = chan_dev // comb
    formed = formed.reshape(chan_devs, beam_dev, comb, part_rows, 2 * samples)
    if part_rows % 16:
        formed = jnp.transpose(formed, (1, 2, 0, 3, 4)).reshape(
            1, beam_dev, comb, chans // comb, 2 * samples
        )
    pieces = [
        dedisperse(formed[:, b], dm_index[b : b + 1], samples, chans) for b in range(beam_dev)
    ]
    return pieces[0] if beam_dev == 1 else jnp.concatenate(pieces, 0)


def solution(mesh):
    return jax.shard_map(
        functools.partial(on_device, mesh.shape["chan"]),
        mesh=mesh,
        in_specs=(
            P(("grp", "chan"), None, None, None),
            P(),
            P("grp"),
            P(("grp", "chan")),
            P("grp"),
        ),
        out_specs=P(("grp", "chan"), None, None, None),
        check_vma=False,
    )
```

```python
import functools
import math

import jax
import jax.numpy as jnp
from jax import lax
from jax.experimental import pallas as pl
from jax.experimental.pallas import tpu as pltpu
from jax.sharding import PartitionSpec as P

TWO_PI = 2.0 * math.pi
BAND_LOW = 0.856
BAND_WIDTH = 0.856
EPSILON = 1e-06
F32 = jnp.float32
BF16 = jnp.bfloat16


def cmul(a, b):
    return (a[0] * b[0] - a[1] * b[1], a[0] * b[1] + a[1] * b[0])


def cadd(a, b):
    return (a[0] + b[0], a[1] + b[1])


def csub(a, b):
    return (a[0] - b[0], a[1] - b[1])


def turn(a, num, den):
    num = num % den
    if num == 0:
        return a
    if 2 * num == den:
        return (-a[0], -a[1])
    if 4 * num == den:
        return (-a[1], a[0])
    if 4 * num == 3 * den:
        return (a[1], -a[0])
    if 8 * num % den == 0:
        root = math.sqrt(0.5)
        plus, minus = (a[0] + a[1]) * root, (a[0] - a[1]) * root
        return {1: (minus, plus), 3: (-plus, minus), 5: (-minus, -plus), 7: (plus, -minus)}[
            8 * num // den
        ]
    cosine, sine = math.cos(TWO_PI * num / den), math.sin(TWO_PI * num / den)
    return (a[0] * cosine - a[1] * sine, a[0] * sine + a[1] * cosine)


def fft_list(values, sign):
    points = len(values)
    if points == 1:
        return values
    if points == 2:
        return [cadd(values[0], values[1]), csub(values[0], values[1])]
    quarter = points // 4
    parts = [fft_list(values[i::4], sign) for i in range(4)]
    out = [None] * points
    for k in range(quarter):
        a, b, c, d = [turn(parts[i][k], sign * i * k, points) for i in range(4)]
        s0, s1 = cadd(a, c), csub(a, c)
        s2, s3 = cadd(b, d), turn(csub(b, d), sign, 4)
        out[k] = cadd(s0, s2)
        out[k + quarter] = cadd(s1, s3)
        out[k + 2 * quarter] = csub(s0, s2)
        out[k + 3 * quarter] = csub(s1, s3)
    return out


def small_phasor(x):
    y = x * x
    cosine = 1.0 - y * (1 / 2 - y * (1 / 24 - y * (1 / 720)))
    return cosine, x * (1.0 - y * (1 / 6 - y * (1 / 120 - y * (1 / 5040))))


def wide_phasor(x):
    quarter = jnp.floor(x * (2.0 / math.pi) + 0.5)
    rest = x - quarter * 1.5703125
    rest = rest - quarter * 4.837512969970703125e-4
    rest = rest - quarter * 7.54978995489188e-8
    y = rest * rest
    cosine = 1.0 - y * (0.5 - y * (1 / 24 - y * (1 / 720 - y * (1 / 40320))))
    sine = rest * (1.0 - y * (1 / 6 - y * (1 / 120 - y * (1 / 5040 - y * (1 / 362880)))))
    turns = quarter.astype(jnp.int32)
    swap = (turns & 1) == 1
    even, odd = jnp.where(swap, sine, cosine), jnp.where(swap, cosine, sine)
    return (
        jnp.where(((turns + 1) & 2) == 2, -even, even),
        jnp.where((turns & 2) == 2, -odd, odd),
    )


def beam_kernel(
    chans, comb, point_ref, delay_hbm, mask_hbm, volt_hbm, out_hbm,
    delay_ref, mask_ref, volt_ref, out_ref, zero_ref, fine_ref, coarse_ref, rows_ref,
    small_sem, volt_sem, out_sem,
):
    part_rows = volt_ref.shape[0]
    beams = out_ref.shape[0]
    dishes = delay_ref.shape[0]
    samples = rows_ref.shape[3]
    chan_dev = part_rows * comb
    group = rows_ref.shape[2] // beams
    group_combs = group // part_rows
    groups = chan_dev // group
    chunks = volt_sem.shape[0]
    ends = [groups * end // 16 for end in (6, 11, 14, 16)] if chunks > 1 else [groups]
    begins = [0] + ends[:-1]

    def volt_copy(g):
        combs = pl.ds(begins[g] * group_combs, (ends[g] - begins[g]) * group_combs)
        return pltpu.make_async_copy(volt_hbm.at[:, combs], volt_ref.at[:, combs], volt_sem.at[g])

    def out_copy(g):
        rows = pl.ds(begins[g] * group, (ends[g] - begins[g]) * group)
        return pltpu.make_async_copy(out_ref.at[:, rows], out_hbm.at[:, rows], out_sem.at[g])

    delay_copy = pltpu.make_async_copy(delay_hbm, delay_ref, small_sem.at[0])
    mask_copy = pltpu.make_async_copy(mask_hbm, mask_ref, small_sem.at[1])
    delay_copy.start()
    mask_copy.start()
    volt_copy(0).start()
    delay_copy.wait()
    mask_copy.wait()
    if chunks > 1:
        volt_copy(1).start()

    table_rows = delay_ref.shape[1]
    place = lax.broadcasted_iota(jnp.int32, (beams, table_rows), 1)
    which = lax.broadcasted_iota(jnp.int32, (beams, table_rows), 0)
    wanted = jnp.zeros((beams, table_rows), jnp.int32)
    for b in range(beams):
        wanted = jnp.where(which == b, point_ref[b], wanted)
    select = (wanted == place).astype(F32).astype(BF16)
    rest, pieces = delay_ref[...], []
    for _ in range(3):
        piece = rest.astype(BF16)
        rest = rest - piece.astype(F32)
        pieces += [piece, piece]
    found = lax.dot_general(
        select,
        jnp.concatenate(pieces, 0),
        (((1,), (1,)), ((), ())),
        preferred_element_type=F32,
    )
    width = 2 * dishes
    tau = (found[:, 2 * width :] + found[:, width : 2 * width]) + found[:, :width]
    first = lax.axis_index("chan") * chan_dev
    frequency = BAND_LOW + BAND_WIDTH * (first.astype(F32) + 0.5) / chans
    angle = (TWO_PI * frequency) * tau
    gain_half = mask_ref[...].astype(F32) / math.sqrt(dishes)
    gain = jnp.concatenate([gain_half, gain_half], 1)
    cosine, sine = wide_phasor(angle)
    cosine, sine = cosine * gain, sine * gain
    left = lax.broadcasted_iota(jnp.int32, (beams, 2 * dishes), 1) < dishes
    zero_ref[0] = jnp.where(left, cosine, sine)
    zero_ref[1] = jnp.where(left, -sine, cosine)
    for table_ref, stride in ((fine_ref, 1), (coarse_ref, comb)):
        shift = (TWO_PI * BAND_WIDTH / chans * stride) * tau
        count = table_ref.shape[0]
        cosine, sine = small_phasor(shift)
        powers = [(jnp.ones_like(tau), jnp.zeros_like(tau)), (cosine, -sine)]
        for k in range(2, count):
            powers.append(cmul(powers[k // 2], powers[k - k // 2]))
        for k in range(count):
            table_ref[k, 0] = powers[k][0]
            table_ref[k, 1] = powers[k][1]

    for g in range(groups):
        if g in begins:
            chunk = begins.index(g)
            volt_copy(chunk).wait()
            if chunk + 2 < chunks:
                volt_copy(chunk + 2).start()
        slot = g % rows_ref.shape[0]
        for i in range(0, group, 2):
            weights, sources = [], []
            for k in range(i, i + 2):
                ja, cb = k % part_rows, g * group_combs + k // part_rows
                if ja == 0:
                    base = cmul((zero_ref[0], zero_ref[1]), (fine_ref[cb, 0], fine_ref[cb, 1]))
                weight = cmul(base, (coarse_ref[ja, 0], coarse_ref[ja, 1]))
                weights.append(jnp.concatenate(weight, 0).astype(BF16))
                sources.append(volt_ref[ja, cb])
            blank = jnp.zeros_like(weights[0])
            stacked = jnp.concatenate(
                [jnp.concatenate([weights[0], blank], 1), jnp.concatenate([blank, weights[1]], 1)], 0
            )
            formed = jnp.dot(stacked, jnp.concatenate(sources, 0), preferred_element_type=F32)
            for k in range(2):
                for p in range(2):
                    rows_ref[slot, p, pl.ds(i + k, beams, stride=group), :] = formed[
                        (2 * k + p) * beams : (2 * k + p + 1) * beams
                    ]
        rows = pl.ds(g * group, group)
        for p in range(2):
            out_ref[:, rows, p * samples : (p + 1) * samples] = (
                rows_ref[slot, p].reshape(beams, group, samples).astype(BF16)
            )
        if g + 1 in ends:
            out_copy(chunk).start()

    for g in range(chunks):
        out_copy(g).wait()


def form_beams(voltages, delays, pointing, dish_mask, chans, comb):
    chan_dev, _, dishes, samples = voltages.shape
    beams = pointing.shape[0]
    part_rows = chan_dev // comb
    group = part_rows * max(1, 16 // part_rows)
    chunks = 4 if (chan_dev // group) % 16 == 0 else 1
    hbm = pl.BlockSpec(memory_space=pltpu.HBM)
    volt = voltages.reshape(part_rows, comb, 2 * dishes, samples)
    return pl.pallas_call(
        functools.partial(beam_kernel, chans, comb),
        out_shape=jax.ShapeDtypeStruct((beams, chan_dev, 2 * samples), BF16),
        in_specs=[pl.BlockSpec(memory_space=pltpu.SMEM), hbm, hbm, hbm],
        out_specs=hbm,
        scratch_shapes=[
            pltpu.VMEM((dishes, delays.shape[0]), F32),
            pltpu.VMEM((1, dishes), jnp.int32),
            pltpu.VMEM(volt.shape, BF16),
            pltpu.VMEM((beams, chan_dev, 2 * samples), BF16),
            pltpu.VMEM((2, beams, 2 * dishes), F32),
            pltpu.VMEM((comb, 2, beams, 2 * dishes), F32),
            pltpu.VMEM((part_rows, 2, beams, 2 * dishes), F32),
            pltpu.VMEM((2, 2, beams * group, samples), F32),
            pltpu.SemaphoreType.DMA((2,)),
            pltpu.SemaphoreType.DMA((chunks,)),
            pltpu.SemaphoreType.DMA((chunks,)),
        ],
        compiler_params=pltpu.CompilerParams(vmem_limit_bytes=60 * 2**20),
        name="form_beams",
    )(pointing, delays.T, dish_mask.reshape(1, dishes), volt)


def phasor(phase, points):
    half = points // 2
    angle = (TWO_PI / points) * ((phase + half) % points - half).astype(F32)
    return jnp.stack([jnp.cos(angle), jnp.sin(angle)], 0)


def chirp_tables(rate, samples, chans):
    length = samples * chans
    low, comb = 2 * samples, chans // (2 * samples)
    f = jnp.arange(samples, dtype=jnp.int32)[None, :]
    shift = 2 * rate * f % chans
    shift_low, shift_high = shift % low, shift // low
    inverse = rate * (2 - rate * rate) % (2 * comb)
    m = jnp.arange(comb, dtype=jnp.int32)[:, None]
    unit = length // (2 * comb)
    c_a = jnp.arange(samples, dtype=jnp.int32)[:, None]
    turn_a = phasor(-(rate * c_a * f % samples), samples)
    turn_b = phasor(-(rate * m * f % (chans // 2)), chans // 2)
    quad = inverse * m * m % (2 * comb) * unit
    place = (m - shift_high) % comb
    wrap = jnp.where(place == 0, comb, 0)
    before = [phasor(quad - (place + beta * wrap) * low * f, length) for beta in range(2)]
    place = rate * m % comb
    quad = inverse * place * place % (2 * comb) * unit
    gauss_phase = -(rate * m * m % (2 * comb)) * unit
    gauss = jnp.sum(phasor(gauss_phase, length), axis=1)
    scale = 2 * samples / (length * math.sqrt(chans))
    turned = phasor(quad + low * place * f + f * shift_low - rate * f * f % length, length)
    after = cmul((turned[0], turned[1]), (gauss[0] * scale, gauss[1] * scale))
    return turn_a, turn_b, jnp.stack(before), jnp.stack(after), shift_low


def time_matrix(samples):
    t = jnp.arange(samples, dtype=jnp.int32)
    cosine, sine = phasor(t[:, None] * t[None, :] % samples, samples)
    return jnp.concatenate(
        [jnp.concatenate([cosine, -sine], 1), jnp.concatenate([sine, cosine], 1)], 0
    ).astype(BF16)


def mix_matrix(samples):
    low = 2 * samples
    n = jnp.arange(low, dtype=jnp.int32)
    cosine, sine = phasor(n[None, :] * n[:, None] % low, low)
    both = jnp.stack([cosine.reshape(low // 8, 8, low), sine.reshape(low // 8, 8, low)], 1)
    return both.reshape(2 * low, low).astype(BF16)


def comb_twiddles(samples, chans):
    low, comb = 2 * samples, chans // (2 * samples)
    n = jnp.arange(low, dtype=jnp.int32)[:, None]
    c_b = jnp.arange(comb, dtype=jnp.int32)[None, :]
    return phasor(n * c_b % chans, chans)


def dedisperse_kernel(
    chans, rate_ref, beam_ref, time_ref, mix_ref, twiddle_ref, turn_a_ref, turn_b_ref, before_ref, after_ref,
    shift_ref, out_hbm, grid_ref, power_ref, scaled_ref, out_ref, moved_ref, out_sem,
):
    samples = turn_a_ref.shape[1]
    low, comb = 2 * samples, grid_ref.shape[0]

    def out_copy(half, high):
        lanes = pl.ds(high * low + half * samples, samples)
        return pltpu.make_async_copy(
            out_ref.at[:, :, lanes], out_hbm.at[0, :, :, lanes], out_sem.at[half, high]
        )

    power_ref[...] = jnp.zeros_like(power_ref)

    for c_b in range(comb):
        beam = beam_ref[:, c_b].reshape(low, 2 * samples)
        wide = beam.astype(F32)
        power_ref[...] += jnp.sum((wide * wide).reshape(low // 8, 8, 2 * samples), 0)
        spectrum = jnp.dot(beam, time_ref[...], preferred_element_type=F32)
        turned = cmul(
            (turn_a_ref[0], turn_a_ref[1]),
            (turn_b_ref[0, pl.ds(c_b, 1), :], turn_b_ref[1, pl.ds(c_b, 1), :]),
        )
        halves = []
        for h in range(2):
            piece = spectrum[h * samples : (h + 1) * samples]
            moved = cmul((piece[:, :samples], piece[:, samples:]), turned)
            halves.append(jnp.concatenate(moved, 1).astype(BF16))
        moved_ref[c_b] = jnp.concatenate(halves, 0)

    for c_b in range(comb):
        moved = moved_ref[c_b]

        mixed = jnp.dot(mix_ref[...], moved, preferred_element_type=F32)
        mixed = mixed.reshape(low // 8, 2, 8, 2 * samples)
        real = mixed[:, 0, :, :samples] - mixed[:, 1, :, samples:]
        imag = mixed[:, 0, :, samples:] + mixed[:, 1, :, :samples]
        values = (real.reshape(low, samples), imag.reshape(low, samples))
        if c_b:
            values = cmul(values, [twiddle_ref[p, :, c_b : c_b + 1] for p in range(2)])
        grid_ref[c_b, 0], grid_ref[c_b, 1] = values

    mean_power = jnp.sum(power_ref[...]) / (samples * chans)
    factor = lax.rsqrt(jnp.full((1, samples), mean_power, F32) + EPSILON)
    for p in range(2):
        scaled_ref[p] = after_ref[p] * factor
    rate = 2 * rate_ref[0] + 1

    def spread(tile):
        rows = pl.ds(pl.multiple_of(tile * 8, 8), 8)
        values = [(grid_ref[c, 0, rows, :], grid_ref[c, 1, rows, :]) for c in range(comb)]
        values = fft_list(values, 1)
        position = tile * 8 + lax.broadcasted_iota(jnp.int32, (8, samples), 0)
        wrapped = position < shift_ref[...]
        for m in range(comb):
            table = [
                jnp.where(wrapped, before_ref[1, p, m : m + 1, :], before_ref[0, p, m : m + 1, :])
                for p in range(2)
            ]
            values[m] = cmul(values[m], table)
        values = fft_list(values, -1)
        for k in range(comb):
            real, imag = cmul(values[k], [scaled_ref[p, k : k + 1, :] for p in range(2)])
            place = lax.rem(rate * k, comb)
            grid_ref[place, 0, rows, :] = real
            grid_ref[place, 1, rows, :] = imag

    def finish(half, high):
        rows = pl.ds(half * samples, samples)
        both = [
            jnp.concatenate([grid_ref[high + i, 0, rows], grid_ref[high + i, 1, rows]], 1)
            for i in range(2)
        ]
        result = lax.dot_general(
            time_ref[...],
            jnp.concatenate(both, 0).astype(BF16),
            (((1,), (1,)), ((), ())),
            preferred_element_type=F32,
        )
        for i in range(2):
            lanes = pl.ds((high + i) * low + half * samples, samples)
            piece = result[:, i * samples : (i + 1) * samples]
            out_ref[0, :, lanes] = piece[:samples]
            out_ref[1, :, lanes] = piece[samples:]

    tiles = samples // 8
    for half in range(2):

        @pl.loop(0, tiles, unroll=1)
        def _(tile):
            spread(half * tiles + tile)

        for first in range(0, comb, 4):
            for high in range(first, first + 4, 2):
                finish(half, high)
            for high in range(first, first + 4):
                out_copy(half, high).start()

    for half in range(2):

        @pl.loop(0, comb)
        def _(high):
            out_copy(half, high).wait()


def dedisperse(beam, trial, samples, chans):
    low, comb = 2 * samples, chans // (2 * samples)
    tables = chirp_tables(2 * trial[0] + 1, samples, chans)
    time_mat = time_matrix(samples)
    mix, twiddles = mix_matrix(samples), comb_twiddles(samples, chans)
    hbm = pl.BlockSpec(memory_space=pltpu.HBM)
    vmem = pl.BlockSpec(memory_space=pltpu.VMEM)
    return pl.pallas_call(
        functools.partial(dedisperse_kernel, chans),
        out_shape=jax.ShapeDtypeStruct((1, 2, samples, chans), F32),
        in_specs=[pl.BlockSpec(memory_space=pltpu.SMEM), vmem, vmem, vmem, vmem] + [vmem] * len(tables),
        out_specs=hbm,
        scratch_shapes=[
            pltpu.VMEM((comb, 2, low, samples), F32),
            pltpu.VMEM((8, 2 * samples), F32),
            pltpu.VMEM((2, comb, samples), F32),
            pltpu.VMEM((2, samples, chans), F32),
            pltpu.VMEM((comb, low, low), BF16),
            pltpu.SemaphoreType.DMA((2, comb)),
        ],
        compiler_params=pltpu.CompilerParams(vmem_limit_bytes=50 * 2**20),
        name="dedisperse",
    )(trial, beam, time_mat, mix, twiddles, *tables)


def on_device(chan_devs, voltages, delays, pointing, dm_index, dish_mask):
    chan_dev, _, _, samples = voltages.shape
    chans = chan_dev * chan_devs
    comb = chans // (2 * samples)
    beam_dev = dm_index.shape[0]
    formed = form_beams(voltages, delays, pointing, dish_mask, chans, comb)
    formed = lax.all_to_all(formed, "chan", split_axis=0, concat_axis=0, tiled=True)
    part_rows = chan_dev // comb
    formed = formed.reshape(chan_devs, beam_dev, comb, part_rows, 2 * samples)
    if part_rows % 16:
        formed = jnp.transpose(formed, (1, 2, 0, 3, 4)).reshape(
            1, beam_dev, comb, chans // comb, 2 * samples
        )
    pieces = [
        dedisperse(formed[:, b], dm_index[b : b + 1], samples, chans) for b in range(beam_dev)
    ]
    return pieces[0] if beam_dev == 1 else jnp.concatenate(pieces, 0)


def solution(mesh):
    return jax.shard_map(
        functools.partial(on_device, mesh.shape["chan"]),
        mesh=mesh,
        in_specs=(
            P(("grp", "chan"), None, None, None),
            P(),
            P("grp"),
            P(("grp", "chan")),
            P("grp"),
        ),
        out_specs=P(("grp", "chan"), None, None, None),
        check_vma=False,
    )
```

```python
import functools
import math

import jax
import jax.numpy as jnp
from jax import lax
from jax.experimental import pallas as pl
from jax.experimental.pallas import tpu as pltpu
from jax.sharding import PartitionSpec as P

TWO_PI = 2.0 * math.pi
BAND_LOW = 0.856
BAND_WIDTH = 0.856
EPSILON = 1e-06
F32 = jnp.float32
BF16 = jnp.bfloat16


def cmul(a, b):
    return (a[0] * b[0] - a[1] * b[1], a[0] * b[1] + a[1] * b[0])


def cadd(a, b):
    return (a[0] + b[0], a[1] + b[1])


def csub(a, b):
    return (a[0] - b[0], a[1] - b[1])


def turn(a, num, den):
    num = num % den
    if num == 0:
        return a
    if 2 * num == den:
        return (-a[0], -a[1])
    if 4 * num == den:
        return (-a[1], a[0])
    if 4 * num == 3 * den:
        return (a[1], -a[0])
    if 8 * num % den == 0:
        root = math.sqrt(0.5)
        plus, minus = (a[0] + a[1]) * root, (a[0] - a[1]) * root
        return {1: (minus, plus), 3: (-plus, minus), 5: (-minus, -plus), 7: (plus, -minus)}[
            8 * num // den
        ]
    cosine, sine = math.cos(TWO_PI * num / den), math.sin(TWO_PI * num / den)
    return (a[0] * cosine - a[1] * sine, a[0] * sine + a[1] * cosine)


def fft_list(values, sign):
    points = len(values)
    if points == 1:
        return values
    if points == 2:
        return [cadd(values[0], values[1]), csub(values[0], values[1])]
    quarter = points // 4
    parts = [fft_list(values[i::4], sign) for i in range(4)]
    out = [None] * points
    for k in range(quarter):
        a, b, c, d = [turn(parts[i][k], sign * i * k, points) for i in range(4)]
        s0, s1 = cadd(a, c), csub(a, c)
        s2, s3 = cadd(b, d), turn(csub(b, d), sign, 4)
        out[k] = cadd(s0, s2)
        out[k + quarter] = cadd(s1, s3)
        out[k + 2 * quarter] = csub(s0, s2)
        out[k + 3 * quarter] = csub(s1, s3)
    return out


def small_phasor(x):
    y = x * x
    cosine = 1.0 - y * (1 / 2 - y * (1 / 24 - y * (1 / 720)))
    return cosine, x * (1.0 - y * (1 / 6 - y * (1 / 120 - y * (1 / 5040))))


def wide_phasor(x):
    quarter = jnp.floor(x * (2.0 / math.pi) + 0.5)
    rest = x - quarter * 1.5703125
    rest = rest - quarter * 4.837512969970703125e-4
    rest = rest - quarter * 7.54978995489188e-8
    y = rest * rest
    cosine = 1.0 - y * (0.5 - y * (1 / 24 - y * (1 / 720 - y * (1 / 40320))))
    sine = rest * (1.0 - y * (1 / 6 - y * (1 / 120 - y * (1 / 5040 - y * (1 / 362880)))))
    turns = quarter.astype(jnp.int32)
    swap = (turns & 1) == 1
    even, odd = jnp.where(swap, sine, cosine), jnp.where(swap, cosine, sine)
    return (
        jnp.where(((turns + 1) & 2) == 2, -even, even),
        jnp.where((turns & 2) == 2, -odd, odd),
    )


def beam_kernel(
    chans, comb, point_ref, delay_hbm, mask_hbm, volt_hbm, out_hbm,
    delay_ref, mask_ref, volt_ref, out_ref, zero_ref, fine_ref, coarse_ref, rows_ref,
    small_sem, volt_sem, out_sem,
):
    part_rows = volt_ref.shape[0]
    beams = out_ref.shape[0]
    dishes = delay_ref.shape[0]
    samples = rows_ref.shape[3]
    chan_dev = part_rows * comb
    group = rows_ref.shape[2] // beams
    group_combs = group // part_rows
    groups = chan_dev // group
    chunks = volt_sem.shape[0]
    ends = [groups * end // 16 for end in (6, 11, 14, 16)] if chunks > 1 else [groups]
    begins = [0] + ends[:-1]

    def volt_copy(g):
        combs = pl.ds(begins[g] * group_combs, (ends[g] - begins[g]) * group_combs)
        return pltpu.make_async_copy(volt_hbm.at[:, combs], volt_ref.at[:, combs], volt_sem.at[g])

    def out_copy(g):
        rows = pl.ds(begins[g] * group, (ends[g] - begins[g]) * group)
        return pltpu.make_async_copy(out_ref.at[:, rows], out_hbm.at[:, rows], out_sem.at[g])

    delay_copy = pltpu.make_async_copy(delay_hbm, delay_ref, small_sem.at[0])
    mask_copy = pltpu.make_async_copy(mask_hbm, mask_ref, small_sem.at[1])
    delay_copy.start()
    mask_copy.start()
    volt_copy(0).start()
    delay_copy.wait()
    mask_copy.wait()
    if chunks > 1:
        volt_copy(1).start()

    table_rows = delay_ref.shape[1]
    place = lax.broadcasted_iota(jnp.int32, (beams, table_rows), 1)
    which = lax.broadcasted_iota(jnp.int32, (beams, table_rows), 0)
    wanted = jnp.zeros((beams, table_rows), jnp.int32)
    for b in range(beams):
        wanted = jnp.where(which == b, point_ref[b], wanted)
    select = (wanted == place).astype(F32).astype(BF16)
    rest, pieces = delay_ref[...], []
    for _ in range(3):
        piece = rest.astype(BF16)
        rest = rest - piece.astype(F32)
        pieces += [piece, piece]
    found = lax.dot_general(
        select,
        jnp.concatenate(pieces, 0),
        (((1,), (1,)), ((), ())),
        preferred_element_type=F32,
    )
    width = 2 * dishes
    tau = (found[:, 2 * width :] + found[:, width : 2 * width]) + found[:, :width]
    first = lax.axis_index("chan") * chan_dev
    frequency = BAND_LOW + BAND_WIDTH * (first.astype(F32) + 0.5) / chans
    angle = (TWO_PI * frequency) * tau
    gain_half = mask_ref[...].astype(F32) / math.sqrt(dishes)
    gain = jnp.concatenate([gain_half, gain_half], 1)
    cosine, sine = wide_phasor(angle)
    cosine, sine = cosine * gain, sine * gain
    left = lax.broadcasted_iota(jnp.int32, (beams, 2 * dishes), 1) < dishes
    zero_ref[0] = jnp.where(left, cosine, sine)
    zero_ref[1] = jnp.where(left, -sine, cosine)
    for table_ref, stride in ((fine_ref, 1), (coarse_ref, comb)):
        shift = (TWO_PI * BAND_WIDTH / chans * stride) * tau
        count = table_ref.shape[0]
        cosine, sine = small_phasor(shift)
        powers = [(jnp.ones_like(tau), jnp.zeros_like(tau)), (cosine, -sine)]
        for k in range(2, count):
            powers.append(cmul(powers[k // 2], powers[k - k // 2]))
        for k in range(count):
            table_ref[k, 0] = powers[k][0]
            table_ref[k, 1] = powers[k][1]

    for g in range(groups):
        if g in begins:
            chunk = begins.index(g)
            volt_copy(chunk).wait()
            if chunk + 2 < chunks:
                volt_copy(chunk + 2).start()
        slot = g % rows_ref.shape[0]
        for i in range(0, group, 2):
            weights, sources = [], []
            for k in range(i, i + 2):
                ja, cb = k % part_rows, g * group_combs + k // part_rows
                if ja == 0:
                    base = cmul((zero_ref[0], zero_ref[1]), (fine_ref[cb, 0], fine_ref[cb, 1]))
                weight = cmul(base, (coarse_ref[ja, 0], coarse_ref[ja, 1]))
                weights.append(jnp.concatenate(weight, 0).astype(BF16))
                sources.append(volt_ref[ja, cb])
            blank = jnp.zeros_like(weights[0])
            stacked = jnp.concatenate(
                [jnp.concatenate([weights[0], blank], 1), jnp.concatenate([blank, weights[1]], 1)], 0
            )
            formed = jnp.dot(stacked, jnp.concatenate(sources, 0), preferred_element_type=F32)
            for k in range(2):
                for p in range(2):
                    rows_ref[slot, p, pl.ds(i + k, beams, stride=group), :] = formed[
                        (2 * k + p) * beams : (2 * k + p + 1) * beams
                    ]
        rows = pl.ds(g * group, group)
        for p in range(2):
            out_ref[:, rows, p * samples : (p + 1) * samples] = (
                rows_ref[slot, p].reshape(beams, group, samples).astype(BF16)
            )
        if g + 1 in ends:
            out_copy(chunk).start()

    for g in range(chunks):
        out_copy(g).wait()


def form_beams(voltages, delays, pointing, dish_mask, chans, comb):
    chan_dev, _, dishes, samples = voltages.shape
    beams = pointing.shape[0]
    part_rows = chan_dev // comb
    group = part_rows * max(1, 16 // part_rows)
    chunks = 4 if (chan_dev // group) % 16 == 0 else 1
    hbm = pl.BlockSpec(memory_space=pltpu.HBM)
    volt = voltages.reshape(part_rows, comb, 2 * dishes, samples)
    return pl.pallas_call(
        functools.partial(beam_kernel, chans, comb),
        out_shape=jax.ShapeDtypeStruct((beams, chan_dev, 2 * samples), BF16),
        in_specs=[pl.BlockSpec(memory_space=pltpu.SMEM), hbm, hbm, hbm],
        out_specs=hbm,
        scratch_shapes=[
            pltpu.VMEM((dishes, delays.shape[0]), F32),
            pltpu.VMEM((1, dishes), jnp.int32),
            pltpu.VMEM(volt.shape, BF16),
            pltpu.VMEM((beams, chan_dev, 2 * samples), BF16),
            pltpu.VMEM((2, beams, 2 * dishes), F32),
            pltpu.VMEM((comb, 2, beams, 2 * dishes), F32),
            pltpu.VMEM((part_rows, 2, beams, 2 * dishes), F32),
            pltpu.VMEM((2, 2, beams * group, samples), F32),
            pltpu.SemaphoreType.DMA((2,)),
            pltpu.SemaphoreType.DMA((chunks,)),
            pltpu.SemaphoreType.DMA((chunks,)),
        ],
        compiler_params=pltpu.CompilerParams(vmem_limit_bytes=60 * 2**20),
        name="form_beams",
    )(pointing, delays.T, dish_mask.reshape(1, dishes), volt)


def phasor(phase, points):
    half = points // 2
    angle = (TWO_PI / points) * ((phase + half) % points - half).astype(F32)
    return jnp.stack([jnp.cos(angle), jnp.sin(angle)], 0)


def chirp_tables(rate, samples, chans):
    length = samples * chans
    low, comb = 2 * samples, chans // (2 * samples)
    f = jnp.arange(samples, dtype=jnp.int32)[None, :]
    shift = 2 * rate * f % chans
    shift_low, shift_high = shift % low, shift // low
    inverse = rate * (2 - rate * rate) % (2 * comb)
    m = jnp.arange(comb, dtype=jnp.int32)[:, None]
    unit = length // (2 * comb)
    c_a = jnp.arange(samples, dtype=jnp.int32)[:, None]
    turn_a = phasor(-(rate * c_a * f % samples), samples)
    turn_b = phasor(-(rate * m * f % (chans // 2)), chans // 2)
    quad = inverse * m * m % (2 * comb) * unit
    place = (m - shift_high) % comb
    wrap = jnp.where(place == 0, comb, 0)
    before = [phasor(quad - (place + beta * wrap) * low * f, length) for beta in range(2)]
    place = rate * m % comb
    quad = inverse * place * place % (2 * comb) * unit
    gauss_phase = -(rate * m * m % (2 * comb)) * unit
    gauss = jnp.sum(phasor(gauss_phase, length), axis=1)
    scale = 2 * samples / (length * math.sqrt(chans))
    turned = phasor(quad + low * place * f + f * shift_low - rate * f * f % length, length)
    after = cmul((turned[0], turned[1]), (gauss[0] * scale, gauss[1] * scale))
    return turn_a, turn_b, jnp.stack(before), jnp.stack(after), shift_low


def time_matrix(samples):
    t = jnp.arange(samples, dtype=jnp.int32)
    cosine, sine = phasor(t[:, None] * t[None, :] % samples, samples)
    return jnp.concatenate(
        [jnp.concatenate([cosine, -sine], 1), jnp.concatenate([sine, cosine], 1)], 0
    ).astype(BF16)


def mix_matrix(samples):
    low = 2 * samples
    n = jnp.arange(low, dtype=jnp.int32)
    cosine, sine = phasor(n[None, :] * n[:, None] % low, low)
    both = jnp.stack([cosine.reshape(low // 8, 8, low), sine.reshape(low // 8, 8, low)], 1)
    return both.reshape(2 * low, low).astype(BF16)


def comb_twiddles(samples, chans):
    low, comb = 2 * samples, chans // (2 * samples)
    n = jnp.arange(low, dtype=jnp.int32)[:, None]
    c_b = jnp.arange(comb, dtype=jnp.int32)[None, :]
    return phasor(n * c_b % chans, chans)


def dedisperse_kernel(
    chans, rate_ref, beam_ref, time_ref, mix_ref, twiddle_ref, turn_a_ref, turn_b_ref, before_ref, after_ref,
    shift_ref, out_hbm, grid_ref, power_ref, scaled_ref, out_ref, moved_ref, out_sem,
):
    samples = turn_a_ref.shape[1]
    low, comb = 2 * samples, grid_ref.shape[0]

    def out_copy(half, high):
        lanes = pl.ds(high * low + half * samples, samples)
        return pltpu.make_async_copy(
            out_ref.at[:, :, lanes], out_hbm.at[0, :, :, lanes], out_sem.at[half, high]
        )

    power_ref[...] = jnp.zeros_like(power_ref)

    for c_b in range(comb):
        beam = beam_ref[:, c_b].reshape(low, 2 * samples)
        wide = beam.astype(F32)
        power_ref[...] += jnp.sum((wide * wide).reshape(low // 8, 8, 2 * samples), 0)
        spectrum = jnp.dot(beam, time_ref[...], preferred_element_type=F32)
        comb_turn = (turn_b_ref[0, pl.ds(c_b, 1), :], turn_b_ref[1, pl.ds(c_b, 1), :])
        halves = []
        for h in range(2):
            piece = spectrum[h * samples : (h + 1) * samples]
            moved = cmul((piece[:, :samples], piece[:, samples:]), (turn_a_ref[0], turn_a_ref[1]))
            moved = cmul(moved, comb_turn)
            halves.append(jnp.concatenate(moved, 1).astype(BF16))
        moved_ref[c_b] = jnp.concatenate(halves, 0)

    mean_power = jnp.sum(power_ref[...]) / (samples * chans)
    factor = lax.rsqrt(jnp.full((1, samples), mean_power, F32) + EPSILON)
    for p in range(2):
        scaled_ref[p] = after_ref[p] * factor
    for c_b in range(comb):
        moved = moved_ref[c_b]

        mixed = jnp.dot(mix_ref[...], moved, preferred_element_type=F32)
        for i in range(low // 8):
            rows = pl.ds(8 * i, 8)
            by_re, by_im = mixed[16 * i : 16 * i + 8], mixed[16 * i + 8 : 16 * i + 16]
            values = (
                by_re[:, :samples] - by_im[:, samples:],
                by_re[:, samples:] + by_im[:, :samples],
            )
            if c_b:
                values = cmul(values, [twiddle_ref[p, rows, c_b : c_b + 1] for p in range(2)])
            grid_ref[c_b, 0, rows], grid_ref[c_b, 1, rows] = values

    rate = 2 * rate_ref[0] + 1

    def spread(tile):
        rows = pl.ds(pl.multiple_of(tile * 8, 8), 8)
        values = [(grid_ref[c, 0, rows, :], grid_ref[c, 1, rows, :]) for c in range(comb)]
        values = fft_list(values, 1)
        position = tile * 8 + lax.broadcasted_iota(jnp.int32, (8, samples), 0)
        wrapped = position < shift_ref[...]
        for m in range(comb):
            table = [
                jnp.where(wrapped, before_ref[1, p, m : m + 1, :], before_ref[0, p, m : m + 1, :])
                for p in range(2)
            ]
            values[m] = cmul(values[m], table)
        values = fft_list(values, -1)
        for k in range(comb):
            real, imag = cmul(values[k], [scaled_ref[p, k : k + 1, :] for p in range(2)])
            place = lax.rem(rate * k, comb)
            grid_ref[place, 0, rows, :] = real
            grid_ref[place, 1, rows, :] = imag

    def finish(half, high):
        rows = pl.ds(half * samples, samples)
        both = [
            jnp.concatenate([grid_ref[high + i, 0, rows], grid_ref[high + i, 1, rows]], 1)
            for i in range(2)
        ]
        result = lax.dot_general(
            time_ref[...],
            jnp.concatenate(both, 0).astype(BF16),
            (((1,), (1,)), ((), ())),
            preferred_element_type=F32,
        )
        for i in range(2):
            lanes = pl.ds((high + i) * low + half * samples, samples)
            piece = result[:, i * samples : (i + 1) * samples]
            out_ref[0, :, lanes] = piece[:samples]
            out_ref[1, :, lanes] = piece[samples:]

    tiles = samples // 8
    for half in range(2):

        @pl.loop(0, tiles, unroll=1)
        def _(tile):
            spread(half * tiles + tile)

        for first in range(0, comb, 4):
            for high in range(first, first + 4, 2):
                finish(half, high)
            for high in range(first, first + 4):
                out_copy(half, high).start()

    for half in range(2):

        @pl.loop(0, comb)
        def _(high):
            out_copy(half, high).wait()


def dedisperse(beam, trial, samples, chans):
    low, comb = 2 * samples, chans // (2 * samples)
    tables = chirp_tables(2 * trial[0] + 1, samples, chans)
    time_mat = time_matrix(samples)
    mix, twiddles = mix_matrix(samples), comb_twiddles(samples, chans)
    hbm = pl.BlockSpec(memory_space=pltpu.HBM)
    vmem = pl.BlockSpec(memory_space=pltpu.VMEM)
    return pl.pallas_call(
        functools.partial(dedisperse_kernel, chans),
        out_shape=jax.ShapeDtypeStruct((1, 2, samples, chans), F32),
        in_specs=[pl.BlockSpec(memory_space=pltpu.SMEM), vmem, vmem, vmem, vmem] + [vmem] * len(tables),
        out_specs=hbm,
        scratch_shapes=[
            pltpu.VMEM((comb, 2, low, samples), F32),
            pltpu.VMEM((8, 2 * samples), F32),
            pltpu.VMEM((2, comb, samples), F32),
            pltpu.VMEM((2, samples, chans), F32),
            pltpu.VMEM((comb, low, low), BF16),
            pltpu.SemaphoreType.DMA((2, comb)),
        ],
        compiler_params=pltpu.CompilerParams(vmem_limit_bytes=50 * 2**20),
        name="dedisperse",
    )(trial, beam, time_mat, mix, twiddles, *tables)


def on_device(chan_devs, voltages, delays, pointing, dm_index, dish_mask):
    chan_dev, _, _, samples = voltages.shape
    chans = chan_dev * chan_devs
    comb = chans // (2 * samples)
    beam_dev = dm_index.shape[0]
    formed = form_beams(voltages, delays, pointing, dish_mask, chans, comb)
    formed = lax.all_to_all(formed, "chan", split_axis=0, concat_axis=0, tiled=True)
    part_rows = chan_dev // comb
    formed = formed.reshape(chan_devs, beam_dev, comb, part_rows, 2 * samples)
    if part_rows % 16:
        formed = jnp.transpose(formed, (1, 2, 0, 3, 4)).reshape(
            1, beam_dev, comb, chans // comb, 2 * samples
        )
    pieces = [
        dedisperse(formed[:, b], dm_index[b : b + 1], samples, chans) for b in range(beam_dev)
    ]
    return pieces[0] if beam_dev == 1 else jnp.concatenate(pieces, 0)


def solution(mesh):
    return jax.shard_map(
        functools.partial(on_device, mesh.shape["chan"]),
        mesh=mesh,
        in_specs=(
            P(("grp", "chan"), None, None, None),
            P(),
            P("grp"),
            P(("grp", "chan")),
            P("grp"),
        ),
        out_specs=P(("grp", "chan"), None, None, None),
        check_vma=False,
    )
```

```python
import functools
import math

import jax
import jax.numpy as jnp
from jax import lax
from jax.experimental import pallas as pl
from jax.experimental.pallas import tpu as pltpu
from jax.sharding import PartitionSpec as P

TWO_PI = 2.0 * math.pi
BAND_LOW = 0.856
BAND_WIDTH = 0.856
EPSILON = 1e-06
F32 = jnp.float32
BF16 = jnp.bfloat16


def cmul(a, b):
    return (a[0] * b[0] - a[1] * b[1], a[0] * b[1] + a[1] * b[0])


def cadd(a, b):
    return (a[0] + b[0], a[1] + b[1])


def csub(a, b):
    return (a[0] - b[0], a[1] - b[1])


def turn(a, num, den):
    num = num % den
    if num == 0:
        return a
    if 2 * num == den:
        return (-a[0], -a[1])
    if 4 * num == den:
        return (-a[1], a[0])
    if 4 * num == 3 * den:
        return (a[1], -a[0])
    if 8 * num % den == 0:
        root = math.sqrt(0.5)
        plus, minus = (a[0] + a[1]) * root, (a[0] - a[1]) * root
        return {1: (minus, plus), 3: (-plus, minus), 5: (-minus, -plus), 7: (plus, -minus)}[
            8 * num // den
        ]
    cosine, sine = math.cos(TWO_PI * num / den), math.sin(TWO_PI * num / den)
    return (a[0] * cosine - a[1] * sine, a[0] * sine + a[1] * cosine)


def fft_list(values, sign):
    points = len(values)
    if points == 1:
        return values
    if points == 2:
        return [cadd(values[0], values[1]), csub(values[0], values[1])]
    quarter = points // 4
    parts = [fft_list(values[i::4], sign) for i in range(4)]
    out = [None] * points
    for k in range(quarter):
        a, b, c, d = [turn(parts[i][k], sign * i * k, points) for i in range(4)]
        s0, s1 = cadd(a, c), csub(a, c)
        s2, s3 = cadd(b, d), turn(csub(b, d), sign, 4)
        out[k] = cadd(s0, s2)
        out[k + quarter] = cadd(s1, s3)
        out[k + 2 * quarter] = csub(s0, s2)
        out[k + 3 * quarter] = csub(s1, s3)
    return out


def small_phasor(x):
    y = x * x
    cosine = 1.0 - y * (1 / 2 - y * (1 / 24 - y * (1 / 720)))
    return cosine, x * (1.0 - y * (1 / 6 - y * (1 / 120 - y * (1 / 5040))))


def wide_phasor(x):
    quarter = jnp.floor(x * (2.0 / math.pi) + 0.5)
    rest = x - quarter * 1.5703125
    rest = rest - quarter * 4.837512969970703125e-4
    rest = rest - quarter * 7.54978995489188e-8
    y = rest * rest
    cosine = 1.0 - y * (0.5 - y * (1 / 24 - y * (1 / 720 - y * (1 / 40320))))
    sine = rest * (1.0 - y * (1 / 6 - y * (1 / 120 - y * (1 / 5040 - y * (1 / 362880)))))
    turns = quarter.astype(jnp.int32)
    swap = (turns & 1) == 1
    even, odd = jnp.where(swap, sine, cosine), jnp.where(swap, cosine, sine)
    return (
        jnp.where(((turns + 1) & 2) == 2, -even, even),
        jnp.where((turns & 2) == 2, -odd, odd),
    )


def beam_kernel(
    chans, comb, point_ref, delay_hbm, mask_hbm, volt_hbm, out_hbm,
    delay_ref, mask_ref, volt_ref, out_ref, zero_ref, fine_ref, coarse_ref, rows_ref,
    small_sem, volt_sem, out_sem,
):
    part_rows = volt_ref.shape[0]
    beams = out_ref.shape[0]
    dishes = delay_ref.shape[0]
    samples = rows_ref.shape[3]
    chan_dev = part_rows * comb
    group = rows_ref.shape[2] // beams
    group_combs = group // part_rows
    groups = chan_dev // group
    chunks = volt_sem.shape[0]
    ends = [groups * end // 16 for end in (5, 10, 14, 16)] if chunks > 1 else [groups]
    begins = [0] + ends[:-1]

    def volt_copy(g):
        combs = pl.ds(begins[g] * group_combs, (ends[g] - begins[g]) * group_combs)
        return pltpu.make_async_copy(volt_hbm.at[:, combs], volt_ref.at[:, combs], volt_sem.at[g])

    def out_copy(g):
        rows = pl.ds(begins[g] * group, (ends[g] - begins[g]) * group)
        return pltpu.make_async_copy(out_ref.at[:, rows], out_hbm.at[:, rows], out_sem.at[g])

    delay_copy = pltpu.make_async_copy(delay_hbm, delay_ref, small_sem.at[0])
    mask_copy = pltpu.make_async_copy(mask_hbm, mask_ref, small_sem.at[1])
    delay_copy.start()
    mask_copy.start()
    volt_copy(0).start()
    delay_copy.wait()
    mask_copy.wait()
    if chunks > 1:
        volt_copy(1).start()

    table_rows = delay_ref.shape[1]
    place = lax.broadcasted_iota(jnp.int32, (beams, table_rows), 1)
    which = lax.broadcasted_iota(jnp.int32, (beams, table_rows), 0)
    wanted = jnp.zeros((beams, table_rows), jnp.int32)
    for b in range(beams):
        wanted = jnp.where(which == b, point_ref[b], wanted)
    select = (wanted == place).astype(F32).astype(BF16)
    rest, pieces = delay_ref[...], []
    for _ in range(3):
        piece = rest.astype(BF16)
        rest = rest - piece.astype(F32)
        pieces += [piece, piece]
    found = lax.dot_general(
        select,
        jnp.concatenate(pieces, 0),
        (((1,), (1,)), ((), ())),
        preferred_element_type=F32,
    )
    width = 2 * dishes
    tau = (found[:, 2 * width :] + found[:, width : 2 * width]) + found[:, :width]
    first = lax.axis_index("chan") * chan_dev
    frequency = BAND_LOW + BAND_WIDTH * (first.astype(F32) + 0.5) / chans
    angle = (TWO_PI * frequency) * tau
    gain_half = mask_ref[...].astype(F32) / math.sqrt(dishes)
    gain = jnp.concatenate([gain_half, gain_half], 1)
    cosine, sine = wide_phasor(angle)
    cosine, sine = cosine * gain, sine * gain
    left = lax.broadcasted_iota(jnp.int32, (beams, 2 * dishes), 1) < dishes
    zero_ref[0] = jnp.where(left, cosine, sine)
    zero_ref[1] = jnp.where(left, -sine, cosine)
    for table_ref, stride in ((fine_ref, 1), (coarse_ref, comb)):
        shift = (TWO_PI * BAND_WIDTH / chans * stride) * tau
        count = table_ref.shape[0]
        cosine, sine = small_phasor(shift)
        powers = [(jnp.ones_like(tau), jnp.zeros_like(tau)), (cosine, -sine)]
        for k in range(2, count):
            powers.append(cmul(powers[k // 2], powers[k - k // 2]))
        for k in range(count):
            table_ref[k, 0] = powers[k][0]
            table_ref[k, 1] = powers[k][1]

    for g in range(groups):
        if g in begins:
            chunk = begins.index(g)
            volt_copy(chunk).wait()
            if chunk == 0:
                for later in range(2, chunks):
                    volt_copy(later).start()
        slot = g % rows_ref.shape[0]
        for i in range(0, group, 2):
            weights, sources = [], []
            for k in range(i, i + 2):
                ja, cb = k % part_rows, g * group_combs + k // part_rows
                if ja == 0:
                    base = cmul((zero_ref[0], zero_ref[1]), (fine_ref[cb, 0], fine_ref[cb, 1]))
                weight = cmul(base, (coarse_ref[ja, 0], coarse_ref[ja, 1]))
                weights.append(jnp.concatenate(weight, 0).astype(BF16))
                sources.append(volt_ref[ja, cb])
            blank = jnp.zeros_like(weights[0])
            stacked = jnp.concatenate(
                [jnp.concatenate([weights[0], blank], 1), jnp.concatenate([blank, weights[1]], 1)], 0
            )
            formed = jnp.dot(stacked, jnp.concatenate(sources, 0), preferred_element_type=F32)
            for k in range(2):
                for p in range(2):
                    rows_ref[slot, p, pl.ds(i + k, beams, stride=group), :] = formed[
                        (2 * k + p) * beams : (2 * k + p + 1) * beams
                    ]
        rows = pl.ds(g * group, group)
        for p in range(2):
            out_ref[:, rows, p * samples : (p + 1) * samples] = (
                rows_ref[slot, p].reshape(beams, group, samples).astype(BF16)
            )
        if g + 1 in ends:
            out_copy(chunk).start()

    for g in range(chunks):
        out_copy(g).wait()


def form_beams(voltages, delays, pointing, dish_mask, chans, comb):
    chan_dev, _, dishes, samples = voltages.shape
    beams = pointing.shape[0]
    part_rows = chan_dev // comb
    group = part_rows * max(1, 16 // part_rows)
    chunks = 4 if (chan_dev // group) % 16 == 0 else 1
    hbm = pl.BlockSpec(memory_space=pltpu.HBM)
    volt = voltages.reshape(part_rows, comb, 2 * dishes, samples)
    return pl.pallas_call(
        functools.partial(beam_kernel, chans, comb),
        out_shape=jax.ShapeDtypeStruct((beams, chan_dev, 2 * samples), BF16),
        in_specs=[pl.BlockSpec(memory_space=pltpu.SMEM), hbm, hbm, hbm],
        out_specs=hbm,
        scratch_shapes=[
            pltpu.VMEM((dishes, delays.shape[0]), F32),
            pltpu.VMEM((1, dishes), jnp.int32),
            pltpu.VMEM(volt.shape, BF16),
            pltpu.VMEM((beams, chan_dev, 2 * samples), BF16),
            pltpu.VMEM((2, beams, 2 * dishes), F32),
            pltpu.VMEM((comb, 2, beams, 2 * dishes), F32),
            pltpu.VMEM((part_rows, 2, beams, 2 * dishes), F32),
            pltpu.VMEM((2, 2, beams * group, samples), F32),
            pltpu.SemaphoreType.DMA((2,)),
            pltpu.SemaphoreType.DMA((chunks,)),
            pltpu.SemaphoreType.DMA((chunks,)),
        ],
        compiler_params=pltpu.CompilerParams(vmem_limit_bytes=60 * 2**20),
        name="form_beams",
    )(pointing, delays.T, dish_mask.reshape(1, dishes), volt)


def phasor(phase, points):
    half = points // 2
    angle = (TWO_PI / points) * ((phase + half) % points - half).astype(F32)
    return jnp.stack([jnp.cos(angle), jnp.sin(angle)], 0)


def chirp_tables(rate, samples, chans):
    length = samples * chans
    low, comb = 2 * samples, chans // (2 * samples)
    f = jnp.arange(samples, dtype=jnp.int32)[None, :]
    shift = 2 * rate * f % chans
    shift_low, shift_high = shift % low, shift // low
    inverse = rate * (2 - rate * rate) % (2 * comb)
    m = jnp.arange(comb, dtype=jnp.int32)[:, None]
    unit = length // (2 * comb)
    c_a = jnp.arange(samples, dtype=jnp.int32)[:, None]
    turn_a = phasor(-(rate * c_a * f % samples), samples)
    turn_b = phasor(-(rate * m * f % (chans // 2)), chans // 2)
    quad = inverse * m * m % (2 * comb) * unit
    place = (m - shift_high) % comb
    wrap = jnp.where(place == 0, comb, 0)
    before = [phasor(quad - (place + beta * wrap) * low * f, length) for beta in range(2)]
    place = rate * m % comb
    quad = inverse * place * place % (2 * comb) * unit
    gauss_phase = -(rate * m * m % (2 * comb)) * unit
    gauss = jnp.sum(phasor(gauss_phase, length), axis=1)
    scale = 2 * samples / (length * math.sqrt(chans))
    turned = phasor(quad + low * place * f + f * shift_low - rate * f * f % length, length)
    after = cmul((turned[0], turned[1]), (gauss[0] * scale, gauss[1] * scale))
    return turn_a, turn_b, jnp.stack(before), jnp.stack(after), shift_low


def time_matrix(samples):
    t = jnp.arange(samples, dtype=jnp.int32)
    cosine, sine = phasor(t[:, None] * t[None, :] % samples, samples)
    return jnp.concatenate(
        [jnp.concatenate([cosine, -sine], 1), jnp.concatenate([sine, cosine], 1)], 0
    ).astype(BF16)


def mix_matrix(samples):
    low = 2 * samples
    n = jnp.arange(low, dtype=jnp.int32)
    cosine, sine = phasor(n[None, :] * n[:, None] % low, low)
    both = jnp.stack([cosine.reshape(low // 8, 8, low), sine.reshape(low // 8, 8, low)], 1)
    return both.reshape(2 * low, low).astype(BF16)


def comb_twiddles(samples, chans):
    low, comb = 2 * samples, chans // (2 * samples)
    n = jnp.arange(low, dtype=jnp.int32)[:, None]
    c_b = jnp.arange(comb, dtype=jnp.int32)[None, :]
    return phasor(n * c_b % chans, chans)


def dedisperse_kernel(
    chans, rate_ref, beam_ref, time_ref, mix_ref, twiddle_ref, turn_a_ref, turn_b_ref, before_ref, after_ref,
    shift_ref, out_hbm, grid_ref, power_ref, scaled_ref, out_ref, moved_ref, out_sem,
):
    samples = turn_a_ref.shape[1]
    low, comb = 2 * samples, grid_ref.shape[0]

    def out_copy(half, high):
        lanes = pl.ds(high * low + half * samples, samples)
        return pltpu.make_async_copy(
            out_ref.at[:, :, lanes], out_hbm.at[0, :, :, lanes], out_sem.at[half, high]
        )

    power_ref[...] = jnp.zeros_like(power_ref)

    for c_b in range(comb):
        beam = beam_ref[:, c_b].reshape(low, 2 * samples)
        wide = beam.astype(F32)
        power_ref[...] += jnp.sum((wide * wide).reshape(low // 8, 8, 2 * samples), 0)
        spectrum = jnp.dot(beam, time_ref[...], preferred_element_type=F32)
        comb_turn = (turn_b_ref[0, pl.ds(c_b, 1), :], turn_b_ref[1, pl.ds(c_b, 1), :])
        halves = []
        for h in range(2):
            piece = spectrum[h * samples : (h + 1) * samples]
            moved = cmul((piece[:, :samples], piece[:, samples:]), (turn_a_ref[0], turn_a_ref[1]))
            moved = cmul(moved, comb_turn)
            halves.append(jnp.concatenate(moved, 1).astype(BF16))
        moved_ref[c_b] = jnp.concatenate(halves, 0)

    mean_power = jnp.sum(power_ref[...]) / (samples * chans)
    factor = lax.rsqrt(jnp.full((1, samples), mean_power, F32) + EPSILON)
    for p in range(2):
        scaled_ref[p] = after_ref[p] * factor
    for c_b in range(comb):
        moved = moved_ref[c_b]

        mixed = jnp.dot(mix_ref[...], moved, preferred_element_type=F32)
        for i in range(low // 8):
            rows = pl.ds(8 * i, 8)
            by_re, by_im = mixed[16 * i : 16 * i + 8], mixed[16 * i + 8 : 16 * i + 16]
            values = (
                by_re[:, :samples] - by_im[:, samples:],
                by_re[:, samples:] + by_im[:, :samples],
            )
            if c_b:
                values = cmul(values, [twiddle_ref[p, rows, c_b : c_b + 1] for p in range(2)])
            grid_ref[c_b, 0, rows], grid_ref[c_b, 1, rows] = values

    rate = 2 * rate_ref[0] + 1

    def spread(tile):
        rows = pl.ds(pl.multiple_of(tile * 8, 8), 8)
        values = [(grid_ref[c, 0, rows, :], grid_ref[c, 1, rows, :]) for c in range(comb)]
        values = fft_list(values, 1)
        position = tile * 8 + lax.broadcasted_iota(jnp.int32, (8, samples), 0)
        wrapped = position < shift_ref[...]
        for m in range(comb):
            table = [
                jnp.where(wrapped, before_ref[1, p, m : m + 1, :], before_ref[0, p, m : m + 1, :])
                for p in range(2)
            ]
            values[m] = cmul(values[m], table)
        values = fft_list(values, -1)
        for k in range(comb):
            real, imag = cmul(values[k], [scaled_ref[p, k : k + 1, :] for p in range(2)])
            place = lax.rem(rate * k, comb)
            grid_ref[place, 0, rows, :] = real
            grid_ref[place, 1, rows, :] = imag

    def finish(half, high):
        rows = pl.ds(half * samples, samples)
        both = [
            jnp.concatenate([grid_ref[high + i, 0, rows], grid_ref[high + i, 1, rows]], 1)
            for i in range(2)
        ]
        result = lax.dot_general(
            time_ref[...],
            jnp.concatenate(both, 0).astype(BF16),
            (((1,), (1,)), ((), ())),
            preferred_element_type=F32,
        )
        for i in range(2):
            lanes = pl.ds((high + i) * low + half * samples, samples)
            piece = result[:, i * samples : (i + 1) * samples]
            out_ref[0, :, lanes] = piece[:samples]
            out_ref[1, :, lanes] = piece[samples:]

    tiles = samples // 8
    for half in range(2):

        @pl.loop(0, tiles, unroll=2)
        def _(tile):
            spread(half * tiles + tile)

        for first in range(0, comb, 4):
            for high in range(first, first + 4, 2):
                finish(half, high)
            for high in range(first, first + 4):
                out_copy(half, high).start()

    for half in range(2):

        @pl.loop(0, comb)
        def _(high):
            out_copy(half, high).wait()


def dedisperse(beam, trial, samples, chans):
    low, comb = 2 * samples, chans // (2 * samples)
    tables = chirp_tables(2 * trial[0] + 1, samples, chans)
    time_mat = time_matrix(samples)
    mix, twiddles = mix_matrix(samples), comb_twiddles(samples, chans)
    hbm = pl.BlockSpec(memory_space=pltpu.HBM)
    vmem = pl.BlockSpec(memory_space=pltpu.VMEM)
    return pl.pallas_call(
        functools.partial(dedisperse_kernel, chans),
        out_shape=jax.ShapeDtypeStruct((1, 2, samples, chans), F32),
        in_specs=[pl.BlockSpec(memory_space=pltpu.SMEM), vmem, vmem, vmem, vmem] + [vmem] * len(tables),
        out_specs=hbm,
        scratch_shapes=[
            pltpu.VMEM((comb, 2, low, samples), F32),
            pltpu.VMEM((8, 2 * samples), F32),
            pltpu.VMEM((2, comb, samples), F32),
            pltpu.VMEM((2, samples, chans), F32),
            pltpu.VMEM((comb, low, low), BF16),
            pltpu.SemaphoreType.DMA((2, comb)),
        ],
        compiler_params=pltpu.CompilerParams(vmem_limit_bytes=50 * 2**20),
        name="dedisperse",
    )(trial, beam, time_mat, mix, twiddles, *tables)


def on_device(chan_devs, voltages, delays, pointing, dm_index, dish_mask):
    chan_dev, _, _, samples = voltages.shape
    chans = chan_dev * chan_devs
    comb = chans // (2 * samples)
    beam_dev = dm_index.shape[0]
    formed = form_beams(voltages, delays, pointing, dish_mask, chans, comb)
    formed = lax.all_to_all(formed, "chan", split_axis=0, concat_axis=0, tiled=True)
    part_rows = chan_dev // comb
    formed = formed.reshape(chan_devs, beam_dev, comb, part_rows, 2 * samples)
    if part_rows % 16:
        formed = jnp.transpose(formed, (1, 2, 0, 3, 4)).reshape(
            1, beam_dev, comb, chans // comb, 2 * samples
        )
    pieces = [
        dedisperse(formed[:, b], dm_index[b : b + 1], samples, chans) for b in range(beam_dev)
    ]
    return pieces[0] if beam_dev == 1 else jnp.concatenate(pieces, 0)


def solution(mesh):
    return jax.shard_map(
        functools.partial(on_device, mesh.shape["chan"]),
        mesh=mesh,
        in_specs=(
            P(("grp", "chan"), None, None, None),
            P(),
            P("grp"),
            P(("grp", "chan")),
            P("grp"),
        ),
        out_specs=P(("grp", "chan"), None, None, None),
        check_vma=False,
    )
```

```python
import functools
import math

import jax
import jax.numpy as jnp
from jax import lax
from jax.experimental import pallas as pl
from jax.experimental.pallas import tpu as pltpu
from jax.sharding import PartitionSpec as P

TWO_PI = 2.0 * math.pi
BAND_LOW = 0.856
BAND_WIDTH = 0.856
EPSILON = 1e-06
F32 = jnp.float32
BF16 = jnp.bfloat16


def cmul(a, b):
    return (a[0] * b[0] - a[1] * b[1], a[0] * b[1] + a[1] * b[0])


def cadd(a, b):
    return (a[0] + b[0], a[1] + b[1])


def csub(a, b):
    return (a[0] - b[0], a[1] - b[1])


def turn(a, num, den):
    num = num % den
    if num == 0:
        return a
    if 2 * num == den:
        return (-a[0], -a[1])
    if 4 * num == den:
        return (-a[1], a[0])
    if 4 * num == 3 * den:
        return (a[1], -a[0])
    if 8 * num % den == 0:
        root = math.sqrt(0.5)
        plus, minus = (a[0] + a[1]) * root, (a[0] - a[1]) * root
        return {1: (minus, plus), 3: (-plus, minus), 5: (-minus, -plus), 7: (plus, -minus)}[
            8 * num // den
        ]
    cosine, sine = math.cos(TWO_PI * num / den), math.sin(TWO_PI * num / den)
    return (a[0] * cosine - a[1] * sine, a[0] * sine + a[1] * cosine)


def fft_list(values, sign):
    points = len(values)
    if points == 1:
        return values
    if points == 2:
        return [cadd(values[0], values[1]), csub(values[0], values[1])]
    quarter = points // 4
    parts = [fft_list(values[i::4], sign) for i in range(4)]
    out = [None] * points
    for k in range(quarter):
        a, b, c, d = [turn(parts[i][k], sign * i * k, points) for i in range(4)]
        s0, s1 = cadd(a, c), csub(a, c)
        s2, s3 = cadd(b, d), turn(csub(b, d), sign, 4)
        out[k] = cadd(s0, s2)
        out[k + quarter] = cadd(s1, s3)
        out[k + 2 * quarter] = csub(s0, s2)
        out[k + 3 * quarter] = csub(s1, s3)
    return out


def small_phasor(x):
    y = x * x
    cosine = 1.0 - y * (1 / 2 - y * (1 / 24 - y * (1 / 720)))
    return cosine, x * (1.0 - y * (1 / 6 - y * (1 / 120 - y * (1 / 5040))))


def wide_phasor(x):
    quarter = jnp.floor(x * (2.0 / math.pi) + 0.5)
    rest = x - quarter * 1.5703125
    rest = rest - quarter * 4.837512969970703125e-4
    rest = rest - quarter * 7.54978995489188e-8
    y = rest * rest
    cosine = 1.0 - y * (0.5 - y * (1 / 24 - y * (1 / 720 - y * (1 / 40320))))
    sine = rest * (1.0 - y * (1 / 6 - y * (1 / 120 - y * (1 / 5040 - y * (1 / 362880)))))
    turns = quarter.astype(jnp.int32)
    swap = (turns & 1) == 1
    even, odd = jnp.where(swap, sine, cosine), jnp.where(swap, cosine, sine)
    return (
        jnp.where(((turns + 1) & 2) == 2, -even, even),
        jnp.where((turns & 2) == 2, -odd, odd),
    )


def beam_kernel(
    chans, comb, point_ref, delay_hbm, mask_hbm, volt_hbm, out_hbm,
    delay_ref, mask_ref, volt_ref, out_ref, zero_ref, fine_ref, coarse_ref, rows_ref,
    small_sem, volt_sem, out_sem,
):
    part_rows = volt_ref.shape[0]
    beams = out_ref.shape[0]
    dishes = delay_ref.shape[0]
    samples = rows_ref.shape[3]
    chan_dev = part_rows * comb
    group = rows_ref.shape[2] // beams
    group_combs = group // part_rows
    groups = chan_dev // group
    chunks = volt_sem.shape[0]
    ends = [groups * end // 16 for end in (5, 10, 14, 16)] if chunks > 1 else [groups]
    begins = [0] + ends[:-1]

    def volt_copy(g):
        combs = pl.ds(begins[g] * group_combs, (ends[g] - begins[g]) * group_combs)
        return pltpu.make_async_copy(volt_hbm.at[:, combs], volt_ref.at[:, combs], volt_sem.at[g])

    def out_copy(g):
        rows = pl.ds(begins[g] * group, (ends[g] - begins[g]) * group)
        return pltpu.make_async_copy(out_ref.at[:, rows], out_hbm.at[:, rows], out_sem.at[g])

    delay_copy = pltpu.make_async_copy(delay_hbm, delay_ref, small_sem.at[0])
    mask_copy = pltpu.make_async_copy(mask_hbm, mask_ref, small_sem.at[1])
    delay_copy.start()
    mask_copy.start()
    volt_copy(0).start()
    delay_copy.wait()
    mask_copy.wait()
    if chunks > 1:
        volt_copy(1).start()

    table_rows = delay_ref.shape[1]
    place = lax.broadcasted_iota(jnp.int32, (beams, table_rows), 1)
    which = lax.broadcasted_iota(jnp.int32, (beams, table_rows), 0)
    wanted = jnp.zeros((beams, table_rows), jnp.int32)
    for b in range(beams):
        wanted = jnp.where(which == b, point_ref[b], wanted)
    select = (wanted == place).astype(F32).astype(BF16)
    rest, pieces = delay_ref[...], []
    for _ in range(3):
        piece = rest.astype(BF16)
        rest = rest - piece.astype(F32)
        pieces += [piece, piece]
    found = lax.dot_general(
        select,
        jnp.concatenate(pieces, 0),
        (((1,), (1,)), ((), ())),
        preferred_element_type=F32,
    )
    width = 2 * dishes
    tau = (found[:, 2 * width :] + found[:, width : 2 * width]) + found[:, :width]
    first = lax.axis_index("chan") * chan_dev
    frequency = BAND_LOW + BAND_WIDTH * (first.astype(F32) + 0.5) / chans
    angle = (TWO_PI * frequency) * tau
    gain_half = mask_ref[...].astype(F32) / math.sqrt(dishes)
    gain = jnp.concatenate([gain_half, gain_half], 1)
    cosine, sine = wide_phasor(angle)
    cosine, sine = cosine * gain, sine * gain
    left = lax.broadcasted_iota(jnp.int32, (beams, 2 * dishes), 1) < dishes
    zero_ref[0] = jnp.where(left, cosine, sine)
    zero_ref[1] = jnp.where(left, -sine, cosine)
    for table_ref, stride in ((fine_ref, 1), (coarse_ref, comb)):
        shift = (TWO_PI * BAND_WIDTH / chans * stride) * tau
        count = table_ref.shape[0]
        cosine, sine = small_phasor(shift)
        powers = [(jnp.ones_like(tau), jnp.zeros_like(tau)), (cosine, -sine)]
        for k in range(2, count):
            powers.append(cmul(powers[k // 2], powers[k - k // 2]))
        for k in range(count):
            table_ref[k, 0] = powers[k][0]
            table_ref[k, 1] = powers[k][1]

    for g in range(groups):
        if g in begins:
            chunk = begins.index(g)
            volt_copy(chunk).wait()
            if chunk == 0:
                for later in range(2, chunks):
                    volt_copy(later).start()
        slot = g % rows_ref.shape[0]
        for i in range(0, group, 2):
            weights, sources = [], []
            for k in range(i, i + 2):
                ja, cb = k % part_rows, g * group_combs + k // part_rows
                if ja == 0:
                    base = cmul((zero_ref[0], zero_ref[1]), (fine_ref[cb, 0], fine_ref[cb, 1]))
                weight = cmul(base, (coarse_ref[ja, 0], coarse_ref[ja, 1]))
                weights.append(jnp.concatenate(weight, 0).astype(BF16))
                sources.append(volt_ref[ja, cb])
            blank = jnp.zeros_like(weights[0])
            stacked = jnp.concatenate(
                [jnp.concatenate([weights[0], blank], 1), jnp.concatenate([blank, weights[1]], 1)], 0
            )
            formed = jnp.dot(stacked, jnp.concatenate(sources, 0), preferred_element_type=F32)
            for k in range(2):
                for p in range(2):
                    rows_ref[slot, p, pl.ds(i + k, beams, stride=group), :] = formed[
                        (2 * k + p) * beams : (2 * k + p + 1) * beams
                    ]
        rows = pl.ds(g * group, group)
        for p in range(2):
            out_ref[:, rows, p * samples : (p + 1) * samples] = (
                rows_ref[slot, p].reshape(beams, group, samples).astype(BF16)
            )
        if g + 1 in ends:
            out_copy(chunk).start()

    for g in range(chunks):
        out_copy(g).wait()


def form_beams(voltages, delays, pointing, dish_mask, chans, comb):
    chan_dev, _, dishes, samples = voltages.shape
    beams = pointing.shape[0]
    part_rows = chan_dev // comb
    group = part_rows * max(1, 16 // part_rows)
    chunks = 4 if (chan_dev // group) % 16 == 0 else 1
    hbm = pl.BlockSpec(memory_space=pltpu.HBM)
    volt = voltages.reshape(part_rows, comb, 2 * dishes, samples)
    return pl.pallas_call(
        functools.partial(beam_kernel, chans, comb),
        out_shape=jax.ShapeDtypeStruct((beams, chan_dev, 2 * samples), BF16),
        in_specs=[pl.BlockSpec(memory_space=pltpu.SMEM), hbm, hbm, hbm],
        out_specs=hbm,
        scratch_shapes=[
            pltpu.VMEM((dishes, delays.shape[0]), F32),
            pltpu.VMEM((1, dishes), jnp.int32),
            pltpu.VMEM(volt.shape, BF16),
            pltpu.VMEM((beams, chan_dev, 2 * samples), BF16),
            pltpu.VMEM((2, beams, 2 * dishes), F32),
            pltpu.VMEM((comb, 2, beams, 2 * dishes), F32),
            pltpu.VMEM((part_rows, 2, beams, 2 * dishes), F32),
            pltpu.VMEM((2, 2, beams * group, samples), F32),
            pltpu.SemaphoreType.DMA((2,)),
            pltpu.SemaphoreType.DMA((chunks,)),
            pltpu.SemaphoreType.DMA((chunks,)),
        ],
        compiler_params=pltpu.CompilerParams(vmem_limit_bytes=60 * 2**20),
        name="form_beams",
    )(pointing, delays.T, dish_mask.reshape(1, dishes), volt)


def phasor(phase, points):
    half = points // 2
    angle = (TWO_PI / points) * ((phase + half) % points - half).astype(F32)
    return jnp.stack([jnp.cos(angle), jnp.sin(angle)], 0)


def chirp_tables(rate, samples, chans):
    length = samples * chans
    low, comb = 2 * samples, chans // (2 * samples)
    f = jnp.arange(samples, dtype=jnp.int32)[None, :]
    shift = 2 * rate * f % chans
    shift_low, shift_high = shift % low, shift // low
    inverse = rate * (2 - rate * rate) % (2 * comb)
    m = jnp.arange(comb, dtype=jnp.int32)[:, None]
    unit = length // (2 * comb)
    c_a = jnp.arange(samples, dtype=jnp.int32)[:, None]
    turn_a = phasor(-(rate * c_a * f % samples), samples)
    turn_b = phasor(-(rate * m * f % (chans // 2)), chans // 2)
    quad = inverse * m * m % (2 * comb) * unit
    place = (m - shift_high) % comb
    wrap = jnp.where(place == 0, comb, 0)
    before = [phasor(quad - (place + beta * wrap) * low * f, length) for beta in range(2)]
    place = rate * m % comb
    quad = inverse * place * place % (2 * comb) * unit
    gauss_phase = -(rate * m * m % (2 * comb)) * unit
    gauss = jnp.sum(phasor(gauss_phase, length), axis=1)
    scale = 2 * samples / (length * math.sqrt(chans))
    turned = phasor(quad + low * place * f + f * shift_low - rate * f * f % length, length)
    after = cmul((turned[0], turned[1]), (gauss[0] * scale, gauss[1] * scale))
    return turn_a, turn_b, jnp.stack(before), jnp.stack(after), shift_low


def time_matrix(samples):
    t = jnp.arange(samples, dtype=jnp.int32)
    cosine, sine = phasor(t[:, None] * t[None, :] % samples, samples)
    return jnp.concatenate(
        [jnp.concatenate([cosine, -sine], 1), jnp.concatenate([sine, cosine], 1)], 0
    ).astype(BF16)


def mix_matrix(samples):
    low = 2 * samples
    n = jnp.arange(low, dtype=jnp.int32)
    cosine, sine = phasor(n[None, :] * n[:, None] % low, low)
    both = jnp.stack([cosine.reshape(low // 8, 8, low), sine.reshape(low // 8, 8, low)], 1)
    return both.reshape(2 * low, low).astype(BF16)


def comb_twiddles(samples, chans):
    low, comb = 2 * samples, chans // (2 * samples)
    n = jnp.arange(low, dtype=jnp.int32)[:, None]
    c_b = jnp.arange(comb, dtype=jnp.int32)[None, :]
    return phasor(n * c_b % chans, chans)


def dedisperse_kernel(
    chans, rate_ref, beam_ref, time_ref, mix_ref, twiddle_ref, turn_a_ref, turn_b_ref, before_ref, after_ref,
    shift_ref, out_hbm, grid_ref, power_ref, scaled_ref, out_ref, moved_ref, out_sem,
):
    samples = turn_a_ref.shape[1]
    low, comb = 2 * samples, grid_ref.shape[0]

    def out_copy(half, high):
        lanes = pl.ds(high * low + half * samples, samples)
        return pltpu.make_async_copy(
            out_ref.at[:, :, lanes], out_hbm.at[0, :, :, lanes], out_sem.at[half, high]
        )

    power_ref[...] = jnp.zeros_like(power_ref)

    for c_b in range(comb):
        beam = beam_ref[:, c_b].reshape(low, 2 * samples)
        wide = beam.astype(F32)
        power_ref[...] += jnp.sum((wide * wide).reshape(low // 8, 8, 2 * samples), 0)
        spectrum = jnp.dot(beam, time_ref[...], preferred_element_type=F32)
        comb_turn = (turn_b_ref[0, pl.ds(c_b, 1), :], turn_b_ref[1, pl.ds(c_b, 1), :])
        halves = []
        for h in range(2):
            piece = spectrum[h * samples : (h + 1) * samples]
            moved = cmul((piece[:, :samples], piece[:, samples:]), (turn_a_ref[0], turn_a_ref[1]))
            moved = cmul(moved, comb_turn)
            halves.append(jnp.concatenate(moved, 1).astype(BF16))
        moved_ref[c_b] = jnp.concatenate(halves, 0)

    mean_power = jnp.sum(power_ref[...]) / (samples * chans)
    factor = lax.rsqrt(jnp.full((1, samples), mean_power, F32) + EPSILON)
    for p in range(2):
        scaled_ref[p] = after_ref[p] * factor
    for first in range(0, comb, 2):
        moved = jnp.concatenate([moved_ref[first], moved_ref[first + 1]], 1)
        mixed = jnp.dot(mix_ref[...], moved, preferred_element_type=F32)
        for c_b in range(first, first + 2):
            at = (c_b - first) * 2 * samples
            mid, end = at + samples, at + 2 * samples
            for i in range(low // 8):
                rows = pl.ds(8 * i, 8)
                by_re, by_im = mixed[16 * i : 16 * i + 8], mixed[16 * i + 8 : 16 * i + 16]
                values = (by_re[:, at:mid] - by_im[:, mid:end], by_re[:, mid:end] + by_im[:, at:mid])
                if c_b:
                    values = cmul(values, [twiddle_ref[p, rows, c_b : c_b + 1] for p in range(2)])
                grid_ref[c_b, 0, rows], grid_ref[c_b, 1, rows] = values

    rate = 2 * rate_ref[0] + 1

    def spread(tile):
        rows = pl.ds(pl.multiple_of(tile * 8, 8), 8)
        values = [(grid_ref[c, 0, rows, :], grid_ref[c, 1, rows, :]) for c in range(comb)]
        values = fft_list(values, 1)
        position = tile * 8 + lax.broadcasted_iota(jnp.int32, (8, samples), 0)
        wrapped = position < shift_ref[...]
        for m in range(comb):
            table = [
                jnp.where(wrapped, before_ref[1, p, m : m + 1, :], before_ref[0, p, m : m + 1, :])
                for p in range(2)
            ]
            values[m] = cmul(values[m], table)
        values = fft_list(values, -1)
        for k in range(comb):
            real, imag = cmul(values[k], [scaled_ref[p, k : k + 1, :] for p in range(2)])
            place = lax.rem(rate * k, comb)
            grid_ref[place, 0, rows, :] = real
            grid_ref[place, 1, rows, :] = imag

    def finish(half, high):
        rows = pl.ds(half * samples, samples)
        both = [
            jnp.concatenate([grid_ref[high + i, 0, rows], grid_ref[high + i, 1, rows]], 1)
            for i in range(2)
        ]
        result = lax.dot_general(
            time_ref[...],
            jnp.concatenate(both, 0).astype(BF16),
            (((1,), (1,)), ((), ())),
            preferred_element_type=F32,
        )
        for i in range(2):
            lanes = pl.ds((high + i) * low + half * samples, samples)
            piece = result[:, i * samples : (i + 1) * samples]
            out_ref[0, :, lanes] = piece[:samples]
            out_ref[1, :, lanes] = piece[samples:]

    tiles = samples // 8
    for half in range(2):

        @pl.loop(0, tiles, unroll=2)
        def _(tile):
            spread(half * tiles + tile)

        for first in range(0, comb, 4):
            for high in range(first, first + 4, 2):
                finish(half, high)
            for high in range(first, first + 4):
                out_copy(half, high).start()

    for half in range(2):

        @pl.loop(0, comb)
        def _(high):
            out_copy(half, high).wait()


def dedisperse(beam, trial, samples, chans):
    low, comb = 2 * samples, chans // (2 * samples)
    tables = chirp_tables(2 * trial[0] + 1, samples, chans)
    time_mat = time_matrix(samples)
    mix, twiddles = mix_matrix(samples), comb_twiddles(samples, chans)
    hbm = pl.BlockSpec(memory_space=pltpu.HBM)
    vmem = pl.BlockSpec(memory_space=pltpu.VMEM)
    return pl.pallas_call(
        functools.partial(dedisperse_kernel, chans),
        out_shape=jax.ShapeDtypeStruct((1, 2, samples, chans), F32),
        in_specs=[pl.BlockSpec(memory_space=pltpu.SMEM), vmem, vmem, vmem, vmem] + [vmem] * len(tables),
        out_specs=hbm,
        scratch_shapes=[
            pltpu.VMEM((comb, 2, low, samples), F32),
            pltpu.VMEM((8, 2 * samples), F32),
            pltpu.VMEM((2, comb, samples), F32),
            pltpu.VMEM((2, samples, chans), F32),
            pltpu.VMEM((comb, low, low), BF16),
            pltpu.SemaphoreType.DMA((2, comb)),
        ],
        compiler_params=pltpu.CompilerParams(vmem_limit_bytes=50 * 2**20),
        name="dedisperse",
    )(trial, beam, time_mat, mix, twiddles, *tables)


def on_device(chan_devs, voltages, delays, pointing, dm_index, dish_mask):
    chan_dev, _, _, samples = voltages.shape
    chans = chan_dev * chan_devs
    comb = chans // (2 * samples)
    beam_dev = dm_index.shape[0]
    formed = form_beams(voltages, delays, pointing, dish_mask, chans, comb)
    formed = lax.all_to_all(formed, "chan", split_axis=0, concat_axis=0, tiled=True)
    part_rows = chan_dev // comb
    formed = formed.reshape(chan_devs, beam_dev, comb, part_rows, 2 * samples)
    if part_rows % 16:
        formed = jnp.transpose(formed, (1, 2, 0, 3, 4)).reshape(
            1, beam_dev, comb, chans // comb, 2 * samples
        )
    pieces = [
        dedisperse(formed[:, b], dm_index[b : b + 1], samples, chans) for b in range(beam_dev)
    ]
    return pieces[0] if beam_dev == 1 else jnp.concatenate(pieces, 0)


def solution(mesh):
    return jax.shard_map(
        functools.partial(on_device, mesh.shape["chan"]),
        mesh=mesh,
        in_specs=(
            P(("grp", "chan"), None, None, None),
            P(),
            P("grp"),
            P(("grp", "chan")),
            P("grp"),
        ),
        out_specs=P(("grp", "chan"), None, None, None),
        check_vma=False,
    )
```
